256 devices in a mesh: seq: 32 (over z_lo, y, core), chan: 8 (over x, z_hi).
Axes of the slice: x: 4, y: 4, z: 8 (z_hi: 2, z_lo: 4; z = z_hi * 4 + z_lo), core: 2. Of those that a mesh axis runs over, the one named last changes fastest.
Arguments:
- query_proj: bfloat16 [128, 131072], P('chan', 'seq'), may hold values from -6 to 6
- key_proj: bfloat16 [128, 131072], P('chan', 'seq'), may hold values from -6 to 6
- value_proj: bfloat16 [128, 131072], P('chan', 'seq'), may hold values from -6 to 6
- filter_taps: float32 [128, 131072], P('chan', 'seq'), may hold values from -1.1 to 1.1
- skip_bias: float32 [128], P('chan'), may hold values from -2.5 to 2.5
Outputs:
- hyena_out: float32 [128, 131072], P(None, ('seq', 'chan'))
The draws below stay inside these ranges and needn't reach their ends.
All inputs are finite; a program needn't handle non-finite values.
Results may differ from the reference program's by a relative error of at most 0.0003.
Values sent between devices are 32-bit elements; how exact they have to be, the bound alone decides.
A program may use at most 64 MiB of HBM per device.

```python
import jax
import jax.numpy as jnp
from jax import lax

CH_DEV = 16
SEQUENCE_LENGTH = 131072
CHANNEL_COUNT = 128
N_CHAN = 8


def draw_filter_taps(key, part):
    key = jax.random.fold_in(key, 11)
    rate_key, kind_key, noise_key, location_random_key, decrease_random_key = jax.random.split(key, 5)
    slow_share = 0.5
    slow_mask = jax.random.uniform(kind_key, (CHANNEL_COUNT,)) < slow_share
    unit_draw = jax.random.uniform(rate_key, (CHANNEL_COUNT,))
    fast_len = 30.0 * jnp.exp(unit_draw * jnp.log(SEQUENCE_LENGTH / 240.0))
    slow_len = 2.0 * SEQUENCE_LENGTH * jnp.exp(unit_draw * jnp.log(4.0))
    decay_len = jnp.where(slow_mask, slow_len, fast_len)
    token_position = jnp.arange(SEQUENCE_LENGTH, dtype=jnp.float32)[None, :]
    spike_locations = jax.random.uniform(location_random_key, (CHANNEL_COUNT, 2)) * SEQUENCE_LENGTH
    spike_decreases = jax.random.uniform(decrease_random_key, (CHANNEL_COUNT, 2), minval=0.5, maxval=0.8)
    filter_envelope = jnp.exp(-token_position / decay_len[:, None])
    filter_envelope = filter_envelope * jnp.where(token_position >= spike_locations[:, 0:1], spike_decreases[:, 0:1], 1.0)
    filter_envelope = filter_envelope * jnp.where(token_position >= spike_locations[:, 1:2], spike_decreases[:, 1:2], 1.0)
    channel_scale = jnp.sqrt(2.0 / jnp.minimum(decay_len, SEQUENCE_LENGTH * 1.0))
    floor_level = jnp.sqrt(0.1 / SEQUENCE_LENGTH)
    magnitude = jnp.maximum(filter_envelope * channel_scale[:, None], floor_level)
    noise_draw = jax.random.truncated_normal(noise_key, -4.0, 4.0, (CHANNEL_COUNT, SEQUENCE_LENGTH))
    return (noise_draw * magnitude).astype(jnp.float32)


def steps_of(own_key, dims, cuts, smallest, top_value):
    def one(position, shards_of):
        heights = jax.random.uniform(jax.random.fold_in(jax.random.fold_in(own_key, 6), position), (shards_of,), jnp.float32, smallest / len(cuts), top_value / len(cuts))
        return jnp.repeat(jnp.exp(heights), dims[position] // shards_of).reshape((-1,) + (1,) * (len(dims) - position - 1))

    loudness = one(*cuts[0])
    for cut in cuts[1:]:
        loudness = loudness * one(*cut)
    return loudness


def scatter_about(rng, shape, spread, limit, cuts=(), held_as=jnp.bfloat16):
    entries = spread * jax.random.normal(rng, shape, jnp.float32)
    if cuts:
        entries = entries * steps_of(rng, shape, cuts, -0.22, 0.18)
    return jnp.clip(entries, -limit, limit).astype(held_as)


def setup_inputs(seed: int = 0) -> dict:
    seeds = jax.random.split(jax.random.key(seed), 6)
    query_proj = scatter_about(seeds[0], (CHANNEL_COUNT, SEQUENCE_LENGTH), 1.0, 6.0, ((0, 8), (1, 32)))
    key_proj = scatter_about(seeds[1], (CHANNEL_COUNT, SEQUENCE_LENGTH), 1.0, 6.0, ((0, 8), (1, 32)))
    value_proj = scatter_about(seeds[2], (CHANNEL_COUNT, SEQUENCE_LENGTH), 1.0, 6.0, ((0, 8), (1, 32)))
    filter_taps = draw_filter_taps(jax.random.fold_in(seeds[5], 71), 0)
    skip_bias = scatter_about(seeds[4], (CHANNEL_COUNT,), 0.5, 2.5, ((0, 8),), jnp.float32)
    return dict(query_proj=query_proj, key_proj=key_proj, value_proj=value_proj, filter_taps=filter_taps, skip_bias=skip_bias)


def reference(query_proj, key_proj, value_proj, filter_taps, skip_bias):
    gated_input = key_proj.astype(jnp.float32) * value_proj.astype(jnp.float32)
    length = 2 * SEQUENCE_LENGTH

    def one_block(pieces):
        signal, filter_row = pieces
        spectrum = jnp.fft.rfft(signal, n=length, axis=-1) * jnp.fft.rfft(filter_row, n=length, axis=-1)
        return jnp.fft.irfft(spectrum, n=length, axis=-1)[:, :SEQUENCE_LENGTH]

    grouped = (gated_input.reshape(N_CHAN, CH_DEV, SEQUENCE_LENGTH), filter_taps.reshape(N_CHAN, CH_DEV, SEQUENCE_LENGTH))
    convolved = lax.map(one_block, grouped).reshape(CHANNEL_COUNT, SEQUENCE_LENGTH).astype(gated_input.dtype)
    return query_proj.astype(jnp.float32) * (convolved + skip_bias[:, None] * gated_input)
```

```python
import math

import jax
import jax.numpy as jnp
import ml_dtypes
import numpy as np
from jax import lax
from jax.experimental import pallas as pl
from jax.experimental.pallas import tpu as pltpu
from jax.sharding import PartitionSpec as P

MESH = pl.DeviceIdType.MESH
F32 = jnp.float32
BF16 = jnp.bfloat16

ROWS = 512
COLS = 256
LENGTH = ROWS * COLS
CHIPS = 16
GROUPS = 8
HALF = ROWS // 2


def halves(table):
    high = table.astype(np.float32).astype(ml_dtypes.bfloat16)
    low = (table - high.astype(np.float64)).astype(np.float32).astype(ml_dtypes.bfloat16)
    return np.stack([high, low], axis=-3)


def tables():
    n1 = np.arange(ROWS, dtype=np.int64)
    n2 = np.arange(COLS, dtype=np.int64)
    angle = 2.0 * math.pi * (n2[:, None] * n2[None, :] % COLS) / COLS
    cos, sin = np.cos(angle), np.sin(angle)
    second = halves(np.block([[cos, -sin], [sin, cos]]))
    second_back = halves(np.block([[cos, sin], [-sin, cos]]))
    first, first_back, twiddle = [], [], []
    for core in range(2):
        k1 = core * HALF + np.arange(HALF, dtype=np.int64)
        angle = 2.0 * math.pi * (n1[None, :] * (4 * k1[:, None] + 1) % (4 * ROWS)) / (4 * ROWS)
        first.append(np.concatenate([np.cos(angle), -np.sin(angle)], axis=0))
        order = []
        for owner in (core, 1 - core):
            for bit in range(2):
                for chip in range(CHIPS):
                    for group in range(GROUPS):
                        order.append(((2 * chip + owner) * GROUPS + group) * 2 + bit)
        back = np.concatenate([np.cos(angle), -np.sin(angle)], axis=0).T / LENGTH
        first_back.append(back[np.array(order)])
        angle = 2.0 * math.pi * (n2[None, :] * (4 * k1[:, None] + 1) % (4 * LENGTH)) / (4 * LENGTH)
        twiddle.append(np.stack([np.cos(angle), -np.sin(angle)]))
    return (
        halves(np.stack(first)),
        second,
        second_back,
        halves(np.stack(first_back)),
        np.stack(twiddle).astype(np.float32),
    )


def split(value):
    high = value.astype(BF16)
    low = (value - high.astype(F32)).astype(BF16)
    return high, low


def dot3(left, right):
    def one(a, b):
        return jnp.dot(a, b, preferred_element_type=F32)

    return one(left[0], right[0]) + (one(left[0], right[1]) + one(left[1], right[0]))


def kernel(
    q_ref, k_ref, v_ref, h_ref, bias_ref, f1_ref, f2_ref, g2_ref, g1_ref, tw_ref, out_ref,
    q_in, k_in, v_in, h_in, f1, f2, g2, g1, tw,
    h_send, u_send, h_all, u_all, q_send, q_all, y_send, y_all, part_send, part_all,
    in_sem, h_out, u_out, h_arrived, u_arrived, twin_out, twin_arrived,
    q_out, q_arrived, part_out, part_arrived, y_out, y_arrived,
):
    s = lax.axis_index("seq")
    g = lax.axis_index("chan")
    core = lax.rem(s, 2)
    chip = lax.div(s, 2)
    twin = s + 1 - 2 * core

    pairs = [
        (h_ref, h_in),
        (k_ref, k_in),
        (v_ref, v_in),
        (q_ref, q_in),
        (f1_ref.at[core], f1),
        (tw_ref.at[core], tw),
        (f2_ref, f2),
        (g2_ref, g2),
        (g1_ref.at[core], g1),
    ]
    loads = [pltpu.make_async_copy(a, b, in_sem.at[n]) for n, (a, b) in enumerate(pairs)]
    for load in loads:
        load.start()

    barrier = pltpu.get_barrier_semaphore()

    @pl.loop(1, CHIPS)
    def _(d):
        pl.semaphore_signal(barrier, inc=1, device_id=(2 * lax.rem(chip + d, CHIPS) + core, g), device_id_type=MESH)

    pl.semaphore_signal(barrier, inc=1, device_id=(twin, g), device_id_type=MESH)

    @pl.loop(1, GROUPS)
    def _(d):
        pl.semaphore_signal(barrier, inc=1, device_id=(s, lax.rem(g + d, GROUPS)), device_id_type=MESH)

    loads[0].wait()
    row = lax.broadcasted_iota(jnp.int32, (CHIPS, 128), 0)
    lane = lax.broadcasted_iota(jnp.int32, (CHIPS, 128), 1)
    direct = jnp.zeros((CHIPS, 128), F32)
    for c in range(CHIPS):
        direct = jnp.where(row == c, bias_ref[c], direct)
    direct = jnp.where((lane == 0) & (s == 0), direct, 0.0)
    h_in[:, 0:128] = h_in[:, 0:128] + direct
    for j in range(32):
        h_send[pl.ds(j, CHIPS, stride=32), :] = h_in[:, 128 * j : 128 * j + 128]
    pl.semaphore_wait(barrier, CHIPS + GROUPS - 1)

    def outward(src, dst, out_sem, arrived):
        @pl.loop(1, CHIPS)
        def _(d):
            to = lax.rem(chip + d, CHIPS)
            pltpu.make_async_remote_copy(
                src_ref=src.at[pl.ds(pl.multiple_of(32 * to, 32), 32)],
                dst_ref=dst.at[pl.ds(pl.multiple_of(32 * s, 32), 32)],
                send_sem=out_sem,
                recv_sem=arrived.at[chip],
                device_id=(2 * to + core, g),
                device_id_type=MESH,
            ).start()

    def to_twin(array, n):
        rows = array.at[pl.ds(pl.multiple_of(32 * (2 * n + core), 32), 32)]
        return rows

    def own(src, dst, sem, arrived):
        dst[pl.ds(pl.multiple_of(32 * s, 32), 32)] = src[pl.ds(pl.multiple_of(32 * chip, 32), 32)]
        rows = to_twin(dst, chip)
        pltpu.make_async_remote_copy(
            src_ref=rows, dst_ref=rows, send_sem=sem, recv_sem=arrived, device_id=(twin, g), device_id_type=MESH
        ).start()

    def pass_on(array, arrived, n):
        @pl.loop(1, CHIPS)
        def _(d):
            source = lax.rem(chip - d + CHIPS, CHIPS)
            rows = to_twin(array, source)
            pltpu.make_async_copy(rows, rows, arrived.at[source]).wait()
            pltpu.make_async_remote_copy(
                src_ref=rows,
                dst_ref=rows,
                send_sem=twin_out.at[n],
                recv_sem=twin_arrived.at[n],
                device_id=(twin, g),
                device_id_type=MESH,
            ).start()

    def wait_bytes(array, sem):
        pltpu.make_async_copy(array, array, sem).wait()

    outward(h_send, h_all, h_out, h_arrived)
    own(h_send, h_all, twin_out.at[0], twin_arrived.at[0])

    loads[1].wait()
    loads[2].wait()
    for j in range(32):
        cols = slice(128 * j, 128 * j + 128)
        u_send[pl.ds(j, CHIPS, stride=32), :] = k_in[:, cols].astype(F32) * v_in[:, cols].astype(F32)
    outward(u_send, u_all, u_out, u_arrived)
    own(u_send, u_all, twin_out.at[1], twin_arrived.at[1])

    loads[3].wait()
    for j in range(GROUPS):
        q_send[16 * j : 16 * j + 16, :] = q_in[:, 512 * j : 512 * j + 512].astype(F32)

    for n in range(4, 9):
        loads[n].wait()

    def forward(array):
        points = jnp.concatenate([array[pl.ds(0, ROWS, stride=2), :], array[pl.ds(1, ROWS, stride=2), :]], axis=1)
        a = dot3((f1[0], f1[1]), split(points))
        re, im = a[:HALF], a[HALF:]
        b = jnp.concatenate([re * tw[0] - im * tw[1], re * tw[1] + im * tw[0]], axis=1)
        return dot3(split(b), (f2[0], f2[1]))

    pass_on(h_all, h_arrived, 0)
    wait_bytes(h_all.at[pl.ds(0, 512)], twin_arrived.at[0])
    hf = forward(h_all)

    pass_on(u_all, u_arrived, 1)

    @pl.loop(1, GROUPS)
    def _(d):
        to = lax.rem(g + d, GROUPS)
        pltpu.make_async_remote_copy(
            src_ref=q_send.at[pl.ds(pl.multiple_of(16 * to, 16), 16)],
            dst_ref=q_all.at[pl.ds(pl.multiple_of(16 * g, 16), 16)],
            send_sem=q_out,
            recv_sem=q_arrived,
            device_id=(s, to),
            device_id_type=MESH,
        ).start()

    q_all[pl.ds(pl.multiple_of(16 * g, 16), 16)] = q_send[pl.ds(pl.multiple_of(16 * g, 16), 16)]

    wait_bytes(u_all.at[pl.ds(0, 512)], twin_arrived.at[1])
    uf = forward(u_all)
    ur, ui, hr, hi = uf[:, :COLS], uf[:, COLS:], hf[:, :COLS], hf[:, COLS:]
    y = jnp.concatenate([ur * hr - ui * hi, ur * hi + ui * hr], axis=1)
    b = dot3(split(y), (g2[0], g2[1]))
    re, im = b[:, :COLS], b[:, COLS:]
    e = split(jnp.concatenate([re * tw[0] + im * tw[1], im * tw[0] - re * tw[1]], axis=0))
    part_send[...] = dot3((g1[0, HALF:], g1[1, HALF:]), e)
    exchange = pltpu.make_async_remote_copy(
        src_ref=part_send,
        dst_ref=part_all,
        send_sem=part_out,
        recv_sem=part_arrived,
        device_id=(twin, g),
        device_id_type=MESH,
    )
    exchange.start()
    mine = dot3((g1[0, :HALF], g1[1, :HALF]), e)
    wait_bytes(q_all.at[pl.ds(0, 112)], q_arrived)
    exchange.wait()
    mine = mine + part_all[...]
    for bit in range(2):
        for side in range(2):
            y_send[:, 2 * bit + side, :] = mine[128 * bit : 128 * bit + 128, 128 * side : 128 * side + 128]

    spot = chip * GROUPS + g
    channel = g * CHIPS + chip

    @pl.loop(1, CHIPS * GROUPS)
    def _(d):
        to = lax.rem(spot + d, CHIPS * GROUPS)
        pltpu.make_async_remote_copy(
            src_ref=y_send.at[to],
            dst_ref=y_all.at[channel],
            send_sem=y_out,
            recv_sem=y_arrived,
            device_id=(2 * lax.div(to, GROUPS) + core, lax.rem(to, GROUPS)),
            device_id_type=MESH,
        ).start()

    y_all[channel] = y_send[spot]
    wait_bytes(y_all.at[pl.ds(0, CHIPS * GROUPS - 1)], y_arrived)
    for j in range(4):
        cols = slice(128 * j, 128 * j + 128)
        out_ref[:, cols] = y_all[:, j, :] * q_all[:, cols]

    wait_bytes(h_send.at[pl.ds(0, 480)], h_out)
    wait_bytes(u_send.at[pl.ds(0, 480)], u_out)
    wait_bytes(h_all.at[pl.ds(0, 512)], twin_out.at[0])
    wait_bytes(u_all.at[pl.ds(0, 512)], twin_out.at[1])
    wait_bytes(q_send.at[pl.ds(0, 112)], q_out)
    wait_bytes(y_send.at[pl.ds(0, CHIPS * GROUPS - 1)], y_out)


def body(query_proj, key_proj, value_proj, filter_taps, skip_bias):
    any_space = pl.BlockSpec(memory_space=pl.ANY)
    dma = pltpu.SemaphoreType.DMA
    consts = [jnp.asarray(t) for t in tables()]
    return pl.pallas_call(
        kernel,
        out_shape=jax.ShapeDtypeStruct((128, 512), F32),
        in_specs=[any_space] * 4 + [pl.BlockSpec(memory_space=pltpu.SMEM)] + [any_space] * 5,
        out_specs=pl.BlockSpec(memory_space=pltpu.VMEM),
        scratch_shapes=[
            pltpu.VMEM((16, 4096), BF16),
            pltpu.VMEM((16, 4096), BF16),
            pltpu.VMEM((16, 4096), BF16),
            pltpu.VMEM((16, 4096), F32),
            pltpu.VMEM((2, ROWS, ROWS), BF16),
            pltpu.VMEM((2, 2 * COLS, 2 * COLS), BF16),
            pltpu.VMEM((2, 2 * COLS, 2 * COLS), BF16),
            pltpu.VMEM((2, ROWS, ROWS), BF16),
            pltpu.VMEM((2, HALF, COLS), F32),
            pltpu.VMEM((512, 128), F32),
            pltpu.VMEM((512, 128), F32),
            pltpu.VMEM((1024, 128), F32),
            pltpu.VMEM((1024, 128), F32),
            pltpu.VMEM((128, 512), F32),
            pltpu.VMEM((128, 512), F32),
            pltpu.VMEM((128, 4, 128), F32),
            pltpu.VMEM((128, 4, 128), F32),
            pltpu.VMEM((HALF, COLS), F32),
            pltpu.VMEM((HALF, COLS), F32),
            dma((9,)),
            dma,
            dma,
            dma((CHIPS,)),
            dma((CHIPS,)),
            dma((2,)),
            dma((2,)),
            dma,
            dma,
            dma,
            dma,
            dma,
            dma,
        ],
        compiler_params=pltpu.CompilerParams(
            collective_id=0, has_side_effects=True, vmem_limit_bytes=48 * 2**20
        ),
        cost_estimate=pl.CostEstimate(flops=2_400_000_000, bytes_accessed=6_000_000, transcendentals=0),
    )(query_proj, key_proj, value_proj, filter_taps, skip_bias, *consts)


def solution(mesh):
    placed = (P("chan", "seq"), P("chan", "seq"), P("chan", "seq"), P("chan", "seq"), P("chan"))
    return jax.shard_map(
        body, mesh=mesh, in_specs=placed, out_specs=P(None, ("seq", "chan")), check_vma=False
    )
```

```python
import math

import jax
import jax.numpy as jnp
import ml_dtypes
import numpy as np
from jax import lax
from jax.experimental import pallas as pl
from jax.experimental.pallas import tpu as pltpu
from jax.sharding import PartitionSpec as P

MESH = pl.DeviceIdType.MESH
F32 = jnp.float32
BF16 = jnp.bfloat16

ROWS = 512
COLS = 256
LENGTH = ROWS * COLS
CHIPS = 16
GROUPS = 8
HALF = ROWS // 2


def halves(table):
    high = table.astype(np.float32).astype(ml_dtypes.bfloat16)
    low = (table - high.astype(np.float64)).astype(np.float32).astype(ml_dtypes.bfloat16)
    return np.stack([high, low], axis=-3)


def tables():
    n1 = np.arange(ROWS, dtype=np.int64)
    n2 = np.arange(COLS, dtype=np.int64)
    angle = 2.0 * math.pi * (n2[:, None] * n2[None, :] % COLS) / COLS
    cos, sin = np.cos(angle), np.sin(angle)
    second = halves(np.block([[cos, -sin], [sin, cos]]))
    second_back = halves(np.block([[cos, sin], [-sin, cos]]))
    first, first_back, twiddle = [], [], []
    for core in range(2):
        k1 = core * HALF + np.arange(HALF, dtype=np.int64)
        angle = 2.0 * math.pi * (n1[None, :] * (4 * k1[:, None] + 1) % (4 * ROWS)) / (4 * ROWS)
        first.append(np.concatenate([np.cos(angle), -np.sin(angle)], axis=0))
        order = []
        for owner in (core, 1 - core):
            for bit in range(2):
                for chip in range(CHIPS):
                    for group in range(GROUPS):
                        order.append(((2 * chip + owner) * GROUPS + group) * 2 + bit)
        back = np.concatenate([np.cos(angle), -np.sin(angle)], axis=0).T / LENGTH
        first_back.append(back[np.array(order)])
        angle = 2.0 * math.pi * (n2[None, :] * (4 * k1[:, None] + 1) % (4 * LENGTH)) / (4 * LENGTH)
        twiddle.append(np.stack([np.cos(angle), -np.sin(angle)]))
    return (
        halves(np.stack(first)),
        second,
        second_back,
        halves(np.stack(first_back)),
        np.stack(twiddle).astype(np.float32),
    )


def split(value):
    high = value.astype(BF16)
    low = (value - high.astype(F32)).astype(BF16)
    return high, low


def dot3(left, right):
    def one(a, b):
        return jnp.dot(a, b, preferred_element_type=F32)

    return one(left[0], right[0]) + (one(left[0], right[1]) + one(left[1], right[0]))


def kernel(
    q_ref, k_ref, v_ref, h_ref, bias_ref, f1_ref, f2_ref, g2_ref, g1_ref, tw_ref, out_ref,
    q_in, k_in, v_in, h_in, f1, f2, g2, g1, tw,
    h_send, u_send, h_all, u_all, q_send, q_all, y_send, y_all, part_send, part_all,
    in_sem, h_out, u_out, h_arrived, u_arrived, twin_out, twin_arrived,
    q_out, q_arrived, part_out, part_arrived, y_out, y_arrived, ready,
):
    s = lax.axis_index("seq")
    g = lax.axis_index("chan")
    core = lax.rem(s, 2)
    chip = lax.div(s, 2)
    twin = s + 1 - 2 * core

    pairs = [
        (h_ref, h_in),
        (k_ref, k_in),
        (v_ref, v_in),
        (q_ref, q_in),
        (f1_ref.at[core], f1),
        (tw_ref.at[core], tw),
        (f2_ref, f2),
        (g2_ref, g2),
        (g1_ref.at[core], g1),
    ]
    loads = [pltpu.make_async_copy(a, b, in_sem.at[n]) for n, (a, b) in enumerate(pairs)]
    loads[0].start()

    barrier = pltpu.get_barrier_semaphore()

    @pl.loop(1, CHIPS)
    def _(d):
        pl.semaphore_signal(barrier, inc=1, device_id=(2 * lax.rem(chip + d, CHIPS) + core, g), device_id_type=MESH)

    pl.semaphore_signal(barrier, inc=1, device_id=(twin, g), device_id_type=MESH)

    @pl.loop(1, GROUPS)
    def _(d):
        pl.semaphore_signal(barrier, inc=1, device_id=(s, lax.rem(g + d, GROUPS)), device_id_type=MESH)

    for load in loads[1:]:
        load.start()

    loads[0].wait()
    row = lax.broadcasted_iota(jnp.int32, (CHIPS, 128), 0)
    lane = lax.broadcasted_iota(jnp.int32, (CHIPS, 128), 1)
    direct = jnp.zeros((CHIPS, 128), F32)
    for c in range(CHIPS):
        direct = jnp.where(row == c, bias_ref[c], direct)
    direct = jnp.where((lane == 0) & (s == 0), direct, 0.0)
    h_in[:, 0:128] = h_in[:, 0:128] + direct
    for j in range(32):
        h_send[pl.ds(j, CHIPS, stride=32), :] = h_in[:, 128 * j : 128 * j + 128]
    pl.semaphore_wait(barrier, CHIPS + GROUPS - 1)

    def outward(src, dst, out_sem, arrived):
        @pl.loop(1, CHIPS)
        def _(d):
            to = chip ^ (CHIPS - d)
            pltpu.make_async_remote_copy(
                src_ref=src.at[pl.ds(pl.multiple_of(32 * to, 32), 32)],
                dst_ref=dst.at[pl.ds(pl.multiple_of(32 * s, 32), 32)],
                send_sem=out_sem,
                recv_sem=arrived.at[chip],
                device_id=(2 * to + core, g),
                device_id_type=MESH,
            ).start()

    def to_twin(array, n):
        rows = array.at[pl.ds(pl.multiple_of(32 * (2 * n + core), 32), 32)]
        return rows

    def own(src, dst, sem, arrived):
        dst[pl.ds(pl.multiple_of(32 * s, 32), 32)] = src[pl.ds(pl.multiple_of(32 * chip, 32), 32)]
        rows = to_twin(dst, chip)
        pltpu.make_async_remote_copy(
            src_ref=rows, dst_ref=rows, send_sem=sem, recv_sem=arrived, device_id=(twin, g), device_id_type=MESH
        ).start()

    def pass_on(array, arrived, n):
        @pl.loop(1, CHIPS)
        def _(d):
            source = chip ^ (CHIPS - d)
            rows = to_twin(array, source)
            pltpu.make_async_copy(rows, rows, arrived.at[source]).wait()
            pltpu.make_async_remote_copy(
                src_ref=rows,
                dst_ref=rows,
                send_sem=twin_out.at[n],
                recv_sem=twin_arrived.at[n],
                device_id=(twin, g),
                device_id_type=MESH,
            ).start()

    def wait_bytes(array, sem):
        pltpu.make_async_copy(array, array, sem).wait()

    outward(h_send, h_all, h_out, h_arrived)

    @pl.loop(1, GROUPS)
    def _(d):
        pl.semaphore_signal(ready, inc=1, device_id=(s, lax.rem(g + d, GROUPS)), device_id_type=MESH)

    own(h_send, h_all, twin_out.at[0], twin_arrived.at[0])

    loads[1].wait()
    loads[2].wait()
    for j in range(32):
        cols = slice(128 * j, 128 * j + 128)
        u_send[pl.ds(j, CHIPS, stride=32), :] = k_in[:, cols].astype(F32) * v_in[:, cols].astype(F32)
    outward(u_send, u_all, u_out, u_arrived)
    own(u_send, u_all, twin_out.at[1], twin_arrived.at[1])

    loads[3].wait()
    for j in range(GROUPS):
        q_send[16 * j : 16 * j + 16, :] = q_in[:, 512 * j : 512 * j + 512].astype(F32)

    for n in range(4, 9):
        loads[n].wait()

    def forward(array):
        points = jnp.concatenate([array[pl.ds(0, ROWS, stride=2), :], array[pl.ds(1, ROWS, stride=2), :]], axis=1)
        a = dot3((f1[0], f1[1]), split(points))
        re, im = a[:HALF], a[HALF:]
        b = jnp.concatenate([re * tw[0] - im * tw[1], re * tw[1] + im * tw[0]], axis=1)
        return dot3(split(b), (f2[0], f2[1]))

    pass_on(h_all, h_arrived, 0)
    wait_bytes(h_all.at[pl.ds(0, 512)], twin_arrived.at[0])
    hf = forward(h_all)

    pass_on(u_all, u_arrived, 1)

    @pl.loop(1, GROUPS)
    def _(d):
        to = lax.rem(g + d, GROUPS)
        pltpu.make_async_remote_copy(
            src_ref=q_send.at[pl.ds(pl.multiple_of(16 * to, 16), 16)],
            dst_ref=q_all.at[pl.ds(pl.multiple_of(16 * g, 16), 16)],
            send_sem=q_out,
            recv_sem=q_arrived,
            device_id=(s, to),
            device_id_type=MESH,
        ).start()

    q_all[pl.ds(pl.multiple_of(16 * g, 16), 16)] = q_send[pl.ds(pl.multiple_of(16 * g, 16), 16)]

    wait_bytes(u_all.at[pl.ds(0, 512)], twin_arrived.at[1])
    uf = forward(u_all)
    ur, ui, hr, hi = uf[:, :COLS], uf[:, COLS:], hf[:, :COLS], hf[:, COLS:]
    y = jnp.concatenate([ur * hr - ui * hi, ur * hi + ui * hr], axis=1)
    b = dot3(split(y), (g2[0], g2[1]))
    re, im = b[:, :COLS], b[:, COLS:]
    e = split(jnp.concatenate([re * tw[0] + im * tw[1], im * tw[0] - re * tw[1]], axis=0))
    part_send[...] = dot3((g1[0, HALF:], g1[1, HALF:]), e)
    exchange = pltpu.make_async_remote_copy(
        src_ref=part_send,
        dst_ref=part_all,
        send_sem=part_out,
        recv_sem=part_arrived,
        device_id=(twin, g),
        device_id_type=MESH,
    )
    exchange.start()
    mine = dot3((g1[0, :HALF], g1[1, :HALF]), e)
    exchange.wait()
    mine = mine + part_all[...]
    for bit in range(2):
        for side in range(2):
            y_send[:, 2 * bit + side, :] = mine[128 * bit : 128 * bit + 128, 128 * side : 128 * side + 128]

    spot = chip * GROUPS + g
    channel = g * CHIPS + chip

    pl.semaphore_wait(ready, GROUPS - 1)

    @pl.loop(1, CHIPS * GROUPS)
    def _(d):
        to = lax.rem(spot + d, CHIPS * GROUPS)
        pltpu.make_async_remote_copy(
            src_ref=y_send.at[to],
            dst_ref=y_all.at[channel],
            send_sem=y_out,
            recv_sem=y_arrived,
            device_id=(2 * lax.div(to, GROUPS) + core, lax.rem(to, GROUPS)),
            device_id_type=MESH,
        ).start()

    y_all[channel] = y_send[spot]
    wait_bytes(q_all.at[pl.ds(0, 112)], q_arrived)
    wait_bytes(y_all.at[pl.ds(0, CHIPS * GROUPS - 1)], y_arrived)
    for j in range(4):
        cols = slice(128 * j, 128 * j + 128)
        out_ref[:, cols] = y_all[:, j, :] * q_all[:, cols]

    wait_bytes(h_send.at[pl.ds(0, 480)], h_out)
    wait_bytes(u_send.at[pl.ds(0, 480)], u_out)
    wait_bytes(h_all.at[pl.ds(0, 512)], twin_out.at[0])
    wait_bytes(u_all.at[pl.ds(0, 512)], twin_out.at[1])
    wait_bytes(q_send.at[pl.ds(0, 112)], q_out)
    wait_bytes(y_send.at[pl.ds(0, CHIPS * GROUPS - 1)], y_out)


def body(query_proj, key_proj, value_proj, filter_taps, skip_bias):
    any_space = pl.BlockSpec(memory_space=pl.ANY)
    dma = pltpu.SemaphoreType.DMA
    consts = [jnp.asarray(t) for t in tables()]
    return pl.pallas_call(
        kernel,
        out_shape=jax.ShapeDtypeStruct((128, 512), F32),
        in_specs=[any_space] * 4 + [pl.BlockSpec(memory_space=pltpu.SMEM)] + [any_space] * 5,
        out_specs=pl.BlockSpec(memory_space=pltpu.VMEM),
        scratch_shapes=[
            pltpu.VMEM((16, 4096), BF16),
            pltpu.VMEM((16, 4096), BF16),
            pltpu.VMEM((16, 4096), BF16),
            pltpu.VMEM((16, 4096), F32),
            pltpu.VMEM((2, ROWS, ROWS), BF16),
            pltpu.VMEM((2, 2 * COLS, 2 * COLS), BF16),
            pltpu.VMEM((2, 2 * COLS, 2 * COLS), BF16),
            pltpu.VMEM((2, ROWS, ROWS), BF16),
            pltpu.VMEM((2, HALF, COLS), F32),
            pltpu.VMEM((512, 128), F32),
            pltpu.VMEM((512, 128), F32),
            pltpu.VMEM((1024, 128), F32),
            pltpu.VMEM((1024, 128), F32),
            pltpu.VMEM((128, 512), F32),
            pltpu.VMEM((128, 512), F32),
            pltpu.VMEM((128, 4, 128), F32),
            pltpu.VMEM((128, 4, 128), F32),
            pltpu.VMEM((HALF, COLS), F32),
            pltpu.VMEM((HALF, COLS), F32),
            dma((9,)),
            dma,
            dma,
            dma((CHIPS,)),
            dma((CHIPS,)),
            dma((2,)),
            dma((2,)),
            dma,
            dma,
            dma,
            dma,
            dma,
            dma,
            pltpu.SemaphoreType.REGULAR,
        ],
        compiler_params=pltpu.CompilerParams(
            collective_id=0, has_side_effects=True, vmem_limit_bytes=62 * 2**20
        ),
        cost_estimate=pl.CostEstimate(flops=2_400_000_000, bytes_accessed=6_000_000, transcendentals=0),
    )(query_proj, key_proj, value_proj, filter_taps, skip_bias, *consts)


def solution(mesh):
    placed = (P("chan", "seq"), P("chan", "seq"), P("chan", "seq"), P("chan", "seq"), P("chan"))
    return jax.shard_map(
        body, mesh=mesh, in_specs=placed, out_specs=P(None, ("seq", "chan")), check_vma=False
    )
```

```python
import math

import jax
import jax.numpy as jnp
import ml_dtypes
import numpy as np
from jax import lax
from jax.experimental import pallas as pl
from jax.experimental.pallas import tpu as pltpu
from jax.sharding import PartitionSpec as P

MESH = pl.DeviceIdType.MESH
F32 = jnp.float32
BF16 = jnp.bfloat16

ROWS = 512
COLS = 256
LENGTH = ROWS * COLS
CHIPS = 16
GROUPS = 8
HALF = ROWS // 2

TAPS_ORDER = [4 * z + y for z in (3, 2, 0, 1) for y in (3, 2, 1, 0) if z + y]
INPUT_ORDER = [4 * z + y for z in (1, 0, 3, 2) for y in (3, 2, 1, 0) if z + y]


def halves(table):
    high = table.astype(np.float32).astype(ml_dtypes.bfloat16)
    low = (table - high.astype(np.float64)).astype(np.float32).astype(ml_dtypes.bfloat16)
    return np.stack([high, low], axis=-3)


def tables():
    n1 = np.arange(ROWS, dtype=np.int64)
    n2 = np.arange(COLS, dtype=np.int64)
    angle = 2.0 * math.pi * (n2[:, None] * n2[None, :] % COLS) / COLS
    cos, sin = np.cos(angle), np.sin(angle)
    second = halves(np.block([[cos, -sin], [sin, cos]]))
    second_back = halves(np.block([[cos, sin], [-sin, cos]]))
    first, first_back, twiddle = [], [], []
    for core in range(2):
        k1 = core * HALF + np.arange(HALF, dtype=np.int64)
        angle = 2.0 * math.pi * (n1[None, :] * (4 * k1[:, None] + 1) % (4 * ROWS)) / (4 * ROWS)
        first.append(np.concatenate([np.cos(angle), -np.sin(angle)], axis=0))
        order = []
        for owner in (core, 1 - core):
            for bit in range(2):
                for chip in range(CHIPS):
                    for group in range(GROUPS):
                        order.append(((2 * chip + owner) * GROUPS + group) * 2 + bit)
        back = np.concatenate([np.cos(angle), -np.sin(angle)], axis=0).T / LENGTH
        first_back.append(back[np.array(order)])
        angle = 2.0 * math.pi * (n2[None, :] * (4 * k1[:, None] + 1) % (4 * LENGTH)) / (4 * LENGTH)
        twiddle.append(np.stack([np.cos(angle), -np.sin(angle)]))
    return (
        halves(np.stack(first)),
        second,
        second_back,
        halves(np.stack(first_back)),
        np.stack(twiddle).astype(np.float32),
    )


def split(value):
    high = value.astype(BF16)
    low = (value - high.astype(F32)).astype(BF16)
    return high, low


def dot3(left, right):
    def one(a, b):
        return jnp.dot(a, b, preferred_element_type=F32)

    return one(left[0], right[0]) + (one(left[0], right[1]) + one(left[1], right[0]))


def kernel(
    q_ref, k_ref, v_ref, h_ref, bias_ref, f1_ref, f2_ref, g2_ref, g1_ref, tw_ref, y_all, q_all,
    q_in, k_in, v_in, h_in, f1, f2, g2, g1, tw,
    h_send, u_send, h_all, u_all, q_send, y_send, part_send, part_all,
    in_sem, h_out, u_out, h_arrived, u_arrived, twin_out, twin_arrived,
    q_out, q_arrived, part_out, part_arrived, y_out, y_arrived, ready, own_sem,
):
    s = lax.axis_index("seq")
    g = lax.axis_index("chan")
    core = lax.rem(s, 2)
    chip = lax.div(s, 2)
    twin = s + 1 - 2 * core

    pairs = [
        (h_ref, h_in),
        (k_ref, k_in),
        (v_ref, v_in),
        (q_ref, q_in),
        (f1_ref.at[core], f1),
        (tw_ref.at[core], tw),
        (f2_ref, f2),
        (g2_ref, g2),
        (g1_ref.at[core], g1),
    ]
    loads = [pltpu.make_async_copy(a, b, in_sem.at[n]) for n, (a, b) in enumerate(pairs)]
    loads[0].start()

    barrier = pltpu.get_barrier_semaphore()

    @pl.loop(1, CHIPS)
    def _(d):
        pl.semaphore_signal(barrier, inc=1, device_id=(2 * lax.rem(chip + d, CHIPS) + core, g), device_id_type=MESH)

    pl.semaphore_signal(barrier, inc=1, device_id=(twin, g), device_id_type=MESH)

    @pl.loop(1, GROUPS)
    def _(d):
        pl.semaphore_signal(barrier, inc=1, device_id=(s, lax.rem(g + d, GROUPS)), device_id_type=MESH)

    for load in loads[1:]:
        load.start()

    loads[0].wait()
    row = lax.broadcasted_iota(jnp.int32, (CHIPS, 128), 0)
    lane = lax.broadcasted_iota(jnp.int32, (CHIPS, 128), 1)
    direct = jnp.zeros((CHIPS, 128), F32)
    for c in range(CHIPS):
        direct = jnp.where(row == c, bias_ref[c], direct)
    direct = jnp.where((lane == 0) & (s == 0), direct, 0.0)
    h_in[:, 0:128] = h_in[:, 0:128] + direct
    for j in range(32):
        h_send[pl.ds(j, CHIPS, stride=32), :] = h_in[:, 128 * j : 128 * j + 128]
    pl.semaphore_wait(barrier, CHIPS + GROUPS - 1)

    def outward(src, dst, out_sem, arrived, order):
        for d in order:
            to = chip ^ d
            pltpu.make_async_remote_copy(
                src_ref=src.at[pl.ds(pl.multiple_of(32 * to, 32), 32)],
                dst_ref=dst.at[pl.ds(pl.multiple_of(32 * s, 32), 32)],
                send_sem=out_sem,
                recv_sem=arrived.at[chip],
                device_id=(2 * to + core, g),
                device_id_type=MESH,
            ).start()

    def to_twin(array, n):
        rows = array.at[pl.ds(pl.multiple_of(32 * (2 * n + core), 32), 32)]
        return rows

    def own(src, dst, sem, arrived):
        dst[pl.ds(pl.multiple_of(32 * s, 32), 32)] = src[pl.ds(pl.multiple_of(32 * chip, 32), 32)]
        rows = to_twin(dst, chip)
        pltpu.make_async_remote_copy(
            src_ref=rows, dst_ref=rows, send_sem=sem, recv_sem=arrived, device_id=(twin, g), device_id_type=MESH
        ).start()

    def pass_on(array, arrived, n, order):
        for d in order:
            source = chip ^ d
            rows = to_twin(array, source)
            pltpu.make_async_copy(rows, rows, arrived.at[source]).wait()
            pltpu.make_async_remote_copy(
                src_ref=rows,
                dst_ref=rows,
                send_sem=twin_out.at[n],
                recv_sem=twin_arrived.at[n],
                device_id=(twin, g),
                device_id_type=MESH,
            ).start()

    def wait_bytes(array, sem):
        pltpu.make_async_copy(array, array, sem).wait()

    outward(h_send, h_all, h_out, h_arrived, TAPS_ORDER)

    @pl.loop(1, GROUPS)
    def _(d):
        pl.semaphore_signal(ready, inc=1, device_id=(s, lax.rem(g + d, GROUPS)), device_id_type=MESH)

    own(h_send, h_all, twin_out.at[0], twin_arrived.at[0])

    loads[1].wait()
    loads[2].wait()
    for j in range(32):
        cols = slice(128 * j, 128 * j + 128)
        u_send[pl.ds(j, CHIPS, stride=32), :] = k_in[:, cols].astype(F32) * v_in[:, cols].astype(F32)
    outward(u_send, u_all, u_out, u_arrived, INPUT_ORDER)
    own(u_send, u_all, twin_out.at[1], twin_arrived.at[1])

    loads[3].wait()
    for j in range(GROUPS):
        q_send[16 * j : 16 * j + 16, :] = q_in[:, 512 * j : 512 * j + 512].astype(F32)

    for n in range(4, 9):
        loads[n].wait()

    def forward(array):
        points = jnp.concatenate([array[pl.ds(0, ROWS, stride=2), :], array[pl.ds(1, ROWS, stride=2), :]], axis=1)
        a = dot3((f1[0], f1[1]), split(points))
        re, im = a[:HALF], a[HALF:]
        b = jnp.concatenate([re * tw[0] - im * tw[1], re * tw[1] + im * tw[0]], axis=1)
        return dot3(split(b), (f2[0], f2[1]))

    pass_on(h_all, h_arrived, 0, TAPS_ORDER)
    wait_bytes(h_all.at[pl.ds(0, 512)], twin_arrived.at[0])
    hf = forward(h_all)

    pass_on(u_all, u_arrived, 1, INPUT_ORDER)

    @pl.loop(1, GROUPS)
    def _(d):
        to = lax.rem(g + d, GROUPS)
        pltpu.make_async_remote_copy(
            src_ref=q_send.at[pl.ds(pl.multiple_of(16 * to, 16), 16)],
            dst_ref=q_all.at[pl.ds(pl.multiple_of(16 * g, 16), 16)],
            send_sem=q_out,
            recv_sem=q_arrived,
            device_id=(s, to),
            device_id_type=MESH,
        ).start()

    q_rows = pl.ds(pl.multiple_of(16 * g, 16), 16)
    q_own = pltpu.make_async_copy(q_send.at[q_rows], q_all.at[q_rows], own_sem.at[0])
    q_own.start()

    wait_bytes(u_all.at[pl.ds(0, 512)], twin_arrived.at[1])
    uf = forward(u_all)
    ur, ui, hr, hi = uf[:, :COLS], uf[:, COLS:], hf[:, :COLS], hf[:, COLS:]
    y = jnp.concatenate([ur * hr - ui * hi, ur * hi + ui * hr], axis=1)
    b = dot3(split(y), (g2[0], g2[1]))
    re, im = b[:, :COLS], b[:, COLS:]
    e = split(jnp.concatenate([re * tw[0] + im * tw[1], im * tw[0] - re * tw[1]], axis=0))
    part_send[...] = dot3((g1[0, HALF:], g1[1, HALF:]), e)
    exchange = pltpu.make_async_remote_copy(
        src_ref=part_send,
        dst_ref=part_all,
        send_sem=part_out,
        recv_sem=part_arrived,
        device_id=(twin, g),
        device_id_type=MESH,
    )
    exchange.start()
    mine = dot3((g1[0, :HALF], g1[1, :HALF]), e)
    exchange.wait()
    mine = mine + part_all[...]
    for bit in range(2):
        for side in range(2):
            y_send[:, 2 * bit + side, :] = mine[128 * bit : 128 * bit + 128, 128 * side : 128 * side + 128]

    spot = chip * GROUPS + g
    channel = g * CHIPS + chip

    pl.semaphore_wait(ready, GROUPS - 1)

    @pl.loop(1, CHIPS * GROUPS)
    def _(d):
        to = lax.rem(spot + d, CHIPS * GROUPS)
        pltpu.make_async_remote_copy(
            src_ref=y_send.at[to],
            dst_ref=y_all.at[channel],
            send_sem=y_out,
            recv_sem=y_arrived,
            device_id=(2 * lax.div(to, GROUPS) + core, lax.rem(to, GROUPS)),
            device_id_type=MESH,
        ).start()

    y_own = pltpu.make_async_copy(y_send.at[spot], y_all.at[channel], own_sem.at[1])
    y_own.start()
    wait_bytes(h_send.at[pl.ds(0, 480)], h_out)
    wait_bytes(u_send.at[pl.ds(0, 480)], u_out)
    wait_bytes(h_all.at[pl.ds(0, 512)], twin_out.at[0])
    wait_bytes(u_all.at[pl.ds(0, 512)], twin_out.at[1])
    wait_bytes(q_send.at[pl.ds(0, 112)], q_out)
    wait_bytes(y_send.at[pl.ds(0, CHIPS * GROUPS - 1)], y_out)
    q_own.wait()
    y_own.wait()
    wait_bytes(q_all.at[pl.ds(0, 112)], q_arrived)
    wait_bytes(y_all.at[pl.ds(0, CHIPS * GROUPS - 1)], y_arrived)


def body(query_proj, key_proj, value_proj, filter_taps, skip_bias):
    any_space = pl.BlockSpec(memory_space=pl.ANY)
    dma = pltpu.SemaphoreType.DMA
    consts = [jnp.asarray(t) for t in tables()]
    y, q = pl.pallas_call(
        kernel,
        out_shape=[jax.ShapeDtypeStruct((128, 4, 128), F32), jax.ShapeDtypeStruct((128, 512), F32)],
        in_specs=[any_space] * 4 + [pl.BlockSpec(memory_space=pltpu.SMEM)] + [any_space] * 5,
        out_specs=[any_space] * 2,
        scratch_shapes=[
            pltpu.VMEM((16, 4096), BF16),
            pltpu.VMEM((16, 4096), BF16),
            pltpu.VMEM((16, 4096), BF16),
            pltpu.VMEM((16, 4096), F32),
            pltpu.VMEM((2, ROWS, ROWS), BF16),
            pltpu.VMEM((2, 2 * COLS, 2 * COLS), BF16),
            pltpu.VMEM((2, 2 * COLS, 2 * COLS), BF16),
            pltpu.VMEM((2, ROWS, ROWS), BF16),
            pltpu.VMEM((2, HALF, COLS), F32),
            pltpu.VMEM((512, 128), F32),
            pltpu.VMEM((512, 128), F32),
            pltpu.VMEM((1024, 128), F32),
            pltpu.VMEM((1024, 128), F32),
            pltpu.VMEM((128, 512), F32),
            pltpu.VMEM((128, 4, 128), F32),
            pltpu.VMEM((HALF, COLS), F32),
            pltpu.VMEM((HALF, COLS), F32),
            dma((9,)),
            dma,
            dma,
            dma((CHIPS,)),
            dma((CHIPS,)),
            dma((2,)),
            dma((2,)),
            dma,
            dma,
            dma,
            dma,
            dma,
            dma,
            pltpu.SemaphoreType.REGULAR,
            dma((2,)),
        ],
        compiler_params=pltpu.CompilerParams(
            collective_id=0, has_side_effects=True, vmem_limit_bytes=62 * 2**20
        ),
        cost_estimate=pl.CostEstimate(flops=2_400_000_000, bytes_accessed=6_000_000, transcendentals=0),
    )(query_proj, key_proj, value_proj, filter_taps, skip_bias, *consts)
    return y.reshape(128, 512) * q


def solution(mesh):
    placed = (P("chan", "seq"), P("chan", "seq"), P("chan", "seq"), P("chan", "seq"), P("chan"))
    return jax.shard_map(
        body, mesh=mesh, in_specs=placed, out_specs=P(None, ("seq", "chan")), check_vma=False
    )
```

```python
import math

import jax
import jax.numpy as jnp
import ml_dtypes
import numpy as np
from jax import lax
from jax.experimental import pallas as pl
from jax.experimental.pallas import tpu as pltpu
from jax.sharding import PartitionSpec as P

MESH = pl.DeviceIdType.MESH
F32 = jnp.float32
BF16 = jnp.bfloat16

ROWS = 512
COLS = 256
LENGTH = ROWS * COLS
CHIPS = 16
GROUPS = 8
HALF = ROWS // 2

TAPS_ORDER = [4 * z + y for z in (3, 2, 0, 1) for y in (3, 2, 1, 0) if z + y]
INPUT_ORDER = [4 * z + y for z in (1, 0, 3, 2) for y in (3, 2, 1, 0) if z + y]


def halves(table):
    high = table.astype(np.float32).astype(ml_dtypes.bfloat16)
    low = (table - high.astype(np.float64)).astype(np.float32).astype(ml_dtypes.bfloat16)
    return np.stack([high, low], axis=-3)


def tables():
    n1 = np.arange(ROWS, dtype=np.int64)
    n2 = np.arange(COLS, dtype=np.int64)
    angle = 2.0 * math.pi * (n2[:, None] * n2[None, :] % COLS) / COLS
    cos, sin = np.cos(angle), np.sin(angle)
    second = halves(np.block([[cos, -sin], [sin, cos]]))
    second_back = halves(np.block([[cos, sin], [-sin, cos]]))
    first, first_back, twiddle = [], [], []
    for core in range(2):
        k1 = core * HALF + np.arange(HALF, dtype=np.int64)
        angle = 2.0 * math.pi * (n1[None, :] * (4 * k1[:, None] + 1) % (4 * ROWS)) / (4 * ROWS)
        first.append(np.concatenate([np.cos(angle), -np.sin(angle)], axis=0))
        order = []
        for owner in (core, 1 - core):
            for bit in range(2):
                for chip in range(CHIPS):
                    for group in range(GROUPS):
                        order.append(((2 * chip + owner) * GROUPS + group) * 2 + bit)
        back = np.concatenate([np.cos(angle), -np.sin(angle)], axis=0).T / LENGTH
        first_back.append(back[np.array(order)])
        angle = 2.0 * math.pi * (n2[None, :] * (4 * k1[:, None] + 1) % (4 * LENGTH)) / (4 * LENGTH)
        twiddle.append(np.stack([np.cos(angle), -np.sin(angle)]))
    return (
        halves(np.stack(first)),
        second,
        second_back,
        halves(np.stack(first_back)),
        np.stack(twiddle).astype(np.float32),
    )


def split(value):
    high = value.astype(BF16)
    low = (value - high.astype(F32)).astype(BF16)
    return high, low


def dot3(left, right):
    def one(a, b):
        return jnp.dot(a, b, preferred_element_type=F32)

    return one(left[0], right[0]) + (one(left[0], right[1]) + one(left[1], right[0]))


def kernel(
    q_ref, k_ref, v_ref, h_ref, b_ref, f1_ref, f2_ref, g2_ref, g1_ref, tw_ref, y_all, q_all,
    q_in, k_in, v_in, h_in, f1, f2, g2, g1, tw,
    h_send, u_send, h_all, u_all, q_send, y_send, part_send, part_all,
    bias_ref, in_sem, h_out, u_out, h_arrived, u_arrived, twin_out, twin_arrived,
    q_out, q_arrived, part_out, part_arrived, y_out, y_arrived, ready, own_sem,
):
    s = lax.axis_index("seq")
    g = lax.axis_index("chan")
    core = lax.rem(s, 2)
    chip = lax.div(s, 2)
    twin = s + 1 - 2 * core

    pairs = [
        (h_ref, h_in),
        (k_ref, k_in),
        (v_ref, v_in),
        (q_ref, q_in),
        (f1_ref.at[core], f1),
        (tw_ref.at[core], tw),
        (f2_ref, f2),
        (g2_ref, g2),
        (g1_ref.at[core], g1),
        (b_ref, bias_ref),
    ]
    loads = [pltpu.make_async_copy(a, b, in_sem.at[n]) for n, (a, b) in enumerate(pairs)]
    loads[0].start()
    loads[9].start()

    barrier = pltpu.get_barrier_semaphore()

    @pl.loop(1, CHIPS)
    def _(d):
        pl.semaphore_signal(barrier, inc=1, device_id=(2 * lax.rem(chip + d, CHIPS) + core, g), device_id_type=MESH)

    pl.semaphore_signal(barrier, inc=1, device_id=(twin, g), device_id_type=MESH)

    @pl.loop(1, GROUPS)
    def _(d):
        pl.semaphore_signal(barrier, inc=1, device_id=(s, lax.rem(g + d, GROUPS)), device_id_type=MESH)

    for load in loads[1:9]:
        load.start()

    loads[0].wait()
    loads[9].wait()
    row = lax.broadcasted_iota(jnp.int32, (CHIPS, 128), 0)
    lane = lax.broadcasted_iota(jnp.int32, (CHIPS, 128), 1)
    direct = jnp.zeros((CHIPS, 128), F32)
    for c in range(CHIPS):
        direct = jnp.where(row == c, bias_ref[c], direct)
    direct = jnp.where((lane == 0) & (s == 0), direct, 0.0)
    h_in[:, 0:128] = h_in[:, 0:128] + direct
    for j in range(32):
        h_send[pl.ds(j, CHIPS, stride=32), :] = h_in[:, 128 * j : 128 * j + 128]
    pl.semaphore_wait(barrier, CHIPS + GROUPS - 1)

    def outward(src, dst, out_sem, arrived, order):
        for d in order:
            to = chip ^ d
            pltpu.make_async_remote_copy(
                src_ref=src.at[pl.ds(pl.multiple_of(32 * to, 32), 32)],
                dst_ref=dst.at[pl.ds(pl.multiple_of(32 * s, 32), 32)],
                send_sem=out_sem,
                recv_sem=arrived.at[chip],
                device_id=(2 * to + core, g),
                device_id_type=MESH,
            ).start()

    def to_twin(array, n):
        rows = array.at[pl.ds(pl.multiple_of(32 * (2 * n + core), 32), 32)]
        return rows

    def own(src, dst, sem, arrived):
        dst[pl.ds(pl.multiple_of(32 * s, 32), 32)] = src[pl.ds(pl.multiple_of(32 * chip, 32), 32)]
        rows = to_twin(dst, chip)
        pltpu.make_async_remote_copy(
            src_ref=rows, dst_ref=rows, send_sem=sem, recv_sem=arrived, device_id=(twin, g), device_id_type=MESH
        ).start()

    def pass_on(array, arrived, n, order):
        for d in order:
            source = chip ^ d
            rows = to_twin(array, source)
            pltpu.make_async_copy(rows, rows, arrived.at[source]).wait()
            pltpu.make_async_remote_copy(
                src_ref=rows,
                dst_ref=rows,
                send_sem=twin_out.at[n],
                recv_sem=twin_arrived.at[n],
                device_id=(twin, g),
                device_id_type=MESH,
            ).start()

    def wait_bytes(array, sem):
        pltpu.make_async_copy(array, array, sem).wait()

    outward(h_send, h_all, h_out, h_arrived, TAPS_ORDER)

    @pl.loop(1, GROUPS)
    def _(d):
        pl.semaphore_signal(ready, inc=1, device_id=(s, lax.rem(g + d, GROUPS)), device_id_type=MESH)

    own(h_send, h_all, twin_out.at[0], twin_arrived.at[0])

    loads[1].wait()
    loads[2].wait()
    for j in range(32):
        cols = slice(128 * j, 128 * j + 128)
        u_send[pl.ds(j, CHIPS, stride=32), :] = k_in[:, cols].astype(F32) * v_in[:, cols].astype(F32)
    outward(u_send, u_all, u_out, u_arrived, INPUT_ORDER)
    own(u_send, u_all, twin_out.at[1], twin_arrived.at[1])

    loads[3].wait()
    for j in range(GROUPS):
        q_send[16 * j : 16 * j + 16, :] = q_in[:, 512 * j : 512 * j + 512].astype(F32)

    def send_query(z_half, first):
        @pl.loop(first, GROUPS // 2)
        def _(d):
            to = 2 * lax.rem(lax.div(g, 2) + d, GROUPS // 2) + z_half
            pltpu.make_async_remote_copy(
                src_ref=q_send.at[pl.ds(pl.multiple_of(16 * to, 16), 16)],
                dst_ref=q_all.at[pl.ds(pl.multiple_of(16 * g, 16), 16)],
                send_sem=q_out,
                recv_sem=q_arrived,
                device_id=(s, to),
                device_id_type=MESH,
            ).start()

    q_rows = pl.ds(pl.multiple_of(16 * g, 16), 16)
    q_own = pltpu.make_async_copy(q_send.at[q_rows], q_all.at[q_rows], own_sem.at[0])
    q_own.start()
    send_query(lax.rem(g, 2), 1)

    for n in range(4, 9):
        loads[n].wait()

    def forward(array):
        points = jnp.concatenate([array[pl.ds(0, ROWS, stride=2), :], array[pl.ds(1, ROWS, stride=2), :]], axis=1)
        a = dot3((f1[0], f1[1]), split(points))
        re, im = a[:HALF], a[HALF:]
        b = jnp.concatenate([re * tw[0] - im * tw[1], re * tw[1] + im * tw[0]], axis=1)
        return dot3(split(b), (f2[0], f2[1]))

    pass_on(h_all, h_arrived, 0, TAPS_ORDER)
    wait_bytes(h_all.at[pl.ds(0, 512)], twin_arrived.at[0])
    hf = forward(h_all)

    pass_on(u_all, u_arrived, 1, INPUT_ORDER)
    send_query(1 - lax.rem(g, 2), 0)

    wait_bytes(u_all.at[pl.ds(0, 512)], twin_arrived.at[1])
    uf = forward(u_all)
    ur, ui, hr, hi = uf[:, :COLS], uf[:, COLS:], hf[:, :COLS], hf[:, COLS:]
    y = jnp.concatenate([ur * hr - ui * hi, ur * hi + ui * hr], axis=1)
    b = dot3(split(y), (g2[0], g2[1]))
    re, im = b[:, :COLS], b[:, COLS:]
    e = split(jnp.concatenate([re * tw[0] + im * tw[1], im * tw[0] - re * tw[1]], axis=0))
    part_send[...] = dot3((g1[0, HALF:], g1[1, HALF:]), e)
    exchange = pltpu.make_async_remote_copy(
        src_ref=part_send,
        dst_ref=part_all,
        send_sem=part_out,
        recv_sem=part_arrived,
        device_id=(twin, g),
        device_id_type=MESH,
    )
    exchange.start()
    mine = dot3((g1[0, :HALF], g1[1, :HALF]), e)
    exchange.wait()
    mine = mine + part_all[...]
    for bit in range(2):
        for side in range(2):
            y_send[:, 2 * bit + side, :] = mine[128 * bit : 128 * bit + 128, 128 * side : 128 * side + 128]

    spot = chip * GROUPS + g
    channel = g * CHIPS + chip

    pl.semaphore_wait(ready, GROUPS - 1)

    @pl.loop(1, CHIPS * GROUPS)
    def _(d):
        to = lax.rem(spot + d, CHIPS * GROUPS)
        pltpu.make_async_remote_copy(
            src_ref=y_send.at[to],
            dst_ref=y_all.at[channel],
            send_sem=y_out,
            recv_sem=y_arrived,
            device_id=(2 * lax.div(to, GROUPS) + core, lax.rem(to, GROUPS)),
            device_id_type=MESH,
        ).start()

    y_own = pltpu.make_async_copy(y_send.at[spot], y_all.at[channel], own_sem.at[1])
    y_own.start()
    wait_bytes(h_send.at[pl.ds(0, 480)], h_out)
    wait_bytes(u_send.at[pl.ds(0, 480)], u_out)
    wait_bytes(h_all.at[pl.ds(0, 512)], twin_out.at[0])
    wait_bytes(u_all.at[pl.ds(0, 512)], twin_out.at[1])
    wait_bytes(q_send.at[pl.ds(0, 112)], q_out)
    wait_bytes(y_send.at[pl.ds(0, CHIPS * GROUPS - 1)], y_out)
    q_own.wait()
    y_own.wait()
    wait_bytes(q_all.at[pl.ds(0, 112)], q_arrived)
    wait_bytes(y_all.at[pl.ds(0, CHIPS * GROUPS - 1)], y_arrived)


def body(query_proj, key_proj, value_proj, filter_taps, skip_bias):
    any_space = pl.BlockSpec(memory_space=pl.ANY)
    dma = pltpu.SemaphoreType.DMA
    consts = [jnp.asarray(t) for t in tables()]
    y, q = pl.pallas_call(
        kernel,
        out_shape=[jax.ShapeDtypeStruct((128, 4, 128), F32), jax.ShapeDtypeStruct((128, 512), F32)],
        in_specs=[any_space] * 10,
        out_specs=[any_space] * 2,
        scratch_shapes=[
            pltpu.VMEM((16, 4096), BF16),
            pltpu.VMEM((16, 4096), BF16),
            pltpu.VMEM((16, 4096), BF16),
            pltpu.VMEM((16, 4096), F32),
            pltpu.VMEM((2, ROWS, ROWS), BF16),
            pltpu.VMEM((2, 2 * COLS, 2 * COLS), BF16),
            pltpu.VMEM((2, 2 * COLS, 2 * COLS), BF16),
            pltpu.VMEM((2, ROWS, ROWS), BF16),
            pltpu.VMEM((2, HALF, COLS), F32),
            pltpu.VMEM((512, 128), F32),
            pltpu.VMEM((512, 128), F32),
            pltpu.VMEM((1024, 128), F32),
            pltpu.VMEM((1024, 128), F32),
            pltpu.VMEM((128, 512), F32),
            pltpu.VMEM((128, 4, 128), F32),
            pltpu.VMEM((HALF, COLS), F32),
            pltpu.VMEM((HALF, COLS), F32),
            pltpu.SMEM((CHIPS,), F32),
            dma((10,)),
            dma,
            dma,
            dma((CHIPS,)),
            dma((CHIPS,)),
            dma((2,)),
            dma((2,)),
            dma,
            dma,
            dma,
            dma,
            dma,
            dma,
            pltpu.SemaphoreType.REGULAR,
            dma((2,)),
        ],
        compiler_params=pltpu.CompilerParams(
            collective_id=0, has_side_effects=True, vmem_limit_bytes=62 * 2**20
        ),
        cost_estimate=pl.CostEstimate(flops=2_400_000_000, bytes_accessed=6_000_000, transcendentals=0),
    )(query_proj, key_proj, value_proj, filter_taps, skip_bias, *consts)
    return y.reshape(128, 512) * q


def solution(mesh):
    placed = (P("chan", "seq"), P("chan", "seq"), P("chan", "seq"), P("chan", "seq"), P("chan"))
    return jax.shard_map(
        body, mesh=mesh, in_specs=placed, out_specs=P(None, ("seq", "chan")), check_vma=False
    )
```

```python
import math

import jax
import jax.numpy as jnp
import ml_dtypes
import numpy as np
from jax import lax
from jax.experimental import pallas as pl
from jax.experimental.pallas import tpu as pltpu
from jax.sharding import PartitionSpec as P

MESH = pl.DeviceIdType.MESH
F32 = jnp.float32
BF16 = jnp.bfloat16

ROWS = 512
COLS = 256
LENGTH = ROWS * COLS
CHIPS = 16
GROUPS = 8
HALF = ROWS // 2

TAPS_ORDER = [4 * z + y for z in (3, 2, 0, 1) for y in (3, 2, 1, 0) if z + y]
INPUT_ORDER = [4 * z + y for z in (1, 0, 3, 2) for y in (3, 2, 1, 0) if z + y]


def halves(table):
    high = table.astype(np.float32).astype(ml_dtypes.bfloat16)
    low = (table - high.astype(np.float64)).astype(np.float32).astype(ml_dtypes.bfloat16)
    return np.stack([high, low], axis=-3)


def tables():
    n1 = np.arange(ROWS, dtype=np.int64)
    n2 = np.arange(COLS, dtype=np.int64)
    angle = 2.0 * math.pi * (n2[:, None] * n2[None, :] % COLS) / COLS
    cos, sin = np.cos(angle), np.sin(angle)
    second = halves(np.block([[cos, -sin], [sin, cos]]))
    second_back = halves(np.block([[cos, sin], [-sin, cos]]))
    first, first_back, twiddle = [], [], []
    for core in range(2):
        k1 = core * HALF + np.arange(HALF, dtype=np.int64)
        angle = 2.0 * math.pi * (n1[None, :] * (4 * k1[:, None] + 1) % (4 * ROWS)) / (4 * ROWS)
        first.append(np.concatenate([np.cos(angle), -np.sin(angle)], axis=0))
        order = []
        for owner in (core, 1 - core):
            for bit in range(2):
                for chip in range(CHIPS):
                    for group in range(GROUPS):
                        order.append(((2 * chip + owner) * GROUPS + group) * 2 + bit)
        back = np.concatenate([np.cos(angle), -np.sin(angle)], axis=0).T / LENGTH
        first_back.append(back[np.array(order)])
        angle = 2.0 * math.pi * (n2[None, :] * (4 * k1[:, None] + 1) % (4 * LENGTH)) / (4 * LENGTH)
        twiddle.append(np.stack([np.cos(angle), -np.sin(angle)]))
    return (
        halves(np.stack(first)),
        second,
        second_back,
        halves(np.stack(first_back)),
        np.stack(twiddle).astype(np.float32),
    )


def split(value):
    high = value.astype(BF16)
    low = (value - high.astype(F32)).astype(BF16)
    return high, low


def dot3(left, right):
    def one(a, b):
        return jnp.dot(a, b, preferred_element_type=F32)

    return one(left[0], right[0]) + (one(left[0], right[1]) + one(left[1], right[0]))


def kernel(
    q_ref, k_ref, v_ref, h_ref, b_ref, f1_ref, f2_ref, g2_ref, g1_ref, tw_ref, y_all, q_all,
    q_in, k_in, v_in, h_in, f1, f2, g2, g1, tw,
    h_send, u_send, h_all, u_all, q_send, y_send, part_send, part_all,
    bias_ref, in_sem, h_out, u_out, h_arrived, u_arrived, twin_out, twin_arrived,
    q_out, q_arrived, part_out, part_arrived, y_out, y_arrived, ready, own_sem,
):
    s = lax.axis_index("seq")
    g = lax.axis_index("chan")
    core = lax.rem(s, 2)
    chip = lax.div(s, 2)
    twin = s + 1 - 2 * core

    pairs = [
        (h_ref, h_in),
        (k_ref, k_in),
        (v_ref, v_in),
        (q_ref, q_in),
        (f1_ref.at[core], f1),
        (tw_ref.at[core], tw),
        (f2_ref, f2),
        (g2_ref, g2),
        (g1_ref.at[core], g1),
        (b_ref, bias_ref),
    ]
    loads = [pltpu.make_async_copy(a, b, in_sem.at[n]) for n, (a, b) in enumerate(pairs)]
    loads[0].start()
    loads[9].start()

    barrier = pltpu.get_barrier_semaphore()

    @pl.loop(1, CHIPS)
    def _(d):
        pl.semaphore_signal(barrier, inc=1, device_id=(2 * lax.rem(chip + d, CHIPS) + core, g), device_id_type=MESH)

    pl.semaphore_signal(barrier, inc=1, device_id=(twin, g), device_id_type=MESH)

    @pl.loop(1, GROUPS)
    def _(d):
        pl.semaphore_signal(barrier, inc=1, device_id=(s, lax.rem(g + d, GROUPS)), device_id_type=MESH)

    for load in loads[1:9]:
        load.start()

    loads[0].wait()
    loads[9].wait()
    row = lax.broadcasted_iota(jnp.int32, (CHIPS, 128), 0)
    lane = lax.broadcasted_iota(jnp.int32, (CHIPS, 128), 1)
    direct = jnp.zeros((CHIPS, 128), F32)
    for c in range(CHIPS):
        direct = jnp.where(row == c, bias_ref[c], direct)
    direct = jnp.where((lane == 0) & (s == 0), direct, 0.0)
    h_in[:, 0:128] = h_in[:, 0:128] + direct
    for j in range(32):
        h_send[pl.ds(j, CHIPS, stride=32), :] = h_in[:, 128 * j : 128 * j + 128]
    pl.semaphore_wait(barrier, CHIPS + GROUPS - 1)

    def outward(src, dst, out_sem, arrived, order):
        for d in order:
            to = chip ^ d
            pltpu.make_async_remote_copy(
                src_ref=src.at[pl.ds(pl.multiple_of(32 * to, 32), 32)],
                dst_ref=dst.at[pl.ds(pl.multiple_of(32 * s, 32), 32)],
                send_sem=out_sem,
                recv_sem=arrived.at[chip],
                device_id=(2 * to + core, g),
                device_id_type=MESH,
            ).start()

    def to_twin(array, n):
        rows = array.at[pl.ds(pl.multiple_of(32 * (2 * n + core), 32), 32)]
        return rows

    def own(src, dst, sem, arrived):
        dst[pl.ds(pl.multiple_of(32 * s, 32), 32)] = src[pl.ds(pl.multiple_of(32 * chip, 32), 32)]
        rows = to_twin(dst, chip)
        pltpu.make_async_remote_copy(
            src_ref=rows, dst_ref=rows, send_sem=sem, recv_sem=arrived, device_id=(twin, g), device_id_type=MESH
        ).start()

    def pass_on(array, arrived, n, order):
        for d in order:
            source = chip ^ d
            rows = to_twin(array, source)
            pltpu.make_async_copy(rows, rows, arrived.at[source]).wait()
            pltpu.make_async_remote_copy(
                src_ref=rows,
                dst_ref=rows,
                send_sem=twin_out.at[n],
                recv_sem=twin_arrived.at[n],
                device_id=(twin, g),
                device_id_type=MESH,
            ).start()

    def wait_bytes(array, sem):
        pltpu.make_async_copy(array, array, sem).wait()

    outward(h_send, h_all, h_out, h_arrived, TAPS_ORDER)

    @pl.loop(1, GROUPS)
    def _(d):
        pl.semaphore_signal(ready, inc=1, device_id=(s, lax.rem(g + d, GROUPS)), device_id_type=MESH)

    own(h_send, h_all, twin_out.at[0], twin_arrived.at[0])

    loads[1].wait()
    loads[2].wait()
    for j in range(32):
        cols = slice(128 * j, 128 * j + 128)
        u_send[pl.ds(j, CHIPS, stride=32), :] = k_in[:, cols].astype(F32) * v_in[:, cols].astype(F32)
    outward(u_send, u_all, u_out, u_arrived, INPUT_ORDER)
    own(u_send, u_all, twin_out.at[1], twin_arrived.at[1])

    loads[3].wait()
    for j in range(GROUPS):
        q_send[16 * j : 16 * j + 16, :] = q_in[:, 512 * j : 512 * j + 512].astype(F32)

    def send_query(z_half, first):
        @pl.loop(first, GROUPS // 2)
        def _(d):
            to = 2 * lax.rem(lax.div(g, 2) + d, GROUPS // 2) + z_half
            pltpu.make_async_remote_copy(
                src_ref=q_send.at[pl.ds(pl.multiple_of(16 * to, 16), 16)],
                dst_ref=q_all.at[pl.ds(pl.multiple_of(16 * g, 16), 16)],
                send_sem=q_out,
                recv_sem=q_arrived,
                device_id=(s, to),
                device_id_type=MESH,
            ).start()

    q_rows = pl.ds(pl.multiple_of(16 * g, 16), 16)
    q_own = pltpu.make_async_copy(q_send.at[q_rows], q_all.at[q_rows], own_sem.at[0])
    q_own.start()
    send_query(lax.rem(g, 2), 1)

    for n in range(4, 9):
        loads[n].wait()

    def forward(array):
        points = jnp.concatenate([array[pl.ds(0, ROWS, stride=2), :], array[pl.ds(1, ROWS, stride=2), :]], axis=1)
        a = dot3((f1[0], f1[1]), split(points))
        re, im = a[:HALF], a[HALF:]
        b = jnp.concatenate([re * tw[0] - im * tw[1], re * tw[1] + im * tw[0]], axis=1)
        return dot3(split(b), (f2[0], f2[1]))

    pass_on(h_all, h_arrived, 0, TAPS_ORDER)
    wait_bytes(h_all.at[pl.ds(0, 512)], twin_arrived.at[0])
    hf = forward(h_all)

    pass_on(u_all, u_arrived, 1, INPUT_ORDER)
    send_query(1 - lax.rem(g, 2), 0)

    wait_bytes(u_all.at[pl.ds(0, 512)], twin_arrived.at[1])
    uf = forward(u_all)
    ur, ui, hr, hi = uf[:, :COLS], uf[:, COLS:], hf[:, :COLS], hf[:, COLS:]
    y = jnp.concatenate([ur * hr - ui * hi, ur * hi + ui * hr], axis=1)
    b = dot3(split(y), (g2[0], g2[1]))
    re, im = b[:, :COLS], b[:, COLS:]
    e = split(jnp.concatenate([re * tw[0] + im * tw[1], im * tw[0] - re * tw[1]], axis=0))
    part_send[...] = dot3((g1[0, HALF:], g1[1, HALF:]), e)
    exchange = pltpu.make_async_remote_copy(
        src_ref=part_send,
        dst_ref=part_all,
        send_sem=part_out,
        recv_sem=part_arrived,
        device_id=(twin, g),
        device_id_type=MESH,
    )
    exchange.start()
    mine = dot3((g1[0, :HALF], g1[1, :HALF]), e)
    exchange.wait()
    mine = mine + part_all[...]
    for bit in range(2):
        for side in range(2):
            y_send[:, 2 * bit + side, :] = mine[128 * bit : 128 * bit + 128, 128 * side : 128 * side + 128]

    spot = chip * GROUPS + g
    channel = g * CHIPS + chip

    pl.semaphore_wait(ready, GROUPS - 1)

    @pl.loop(1, CHIPS * GROUPS)
    def _(d):
        to = lax.rem(spot + d, CHIPS * GROUPS)
        pltpu.make_async_remote_copy(
            src_ref=y_send.at[to],
            dst_ref=y_all.at[channel],
            send_sem=y_out,
            recv_sem=y_arrived,
            device_id=(2 * lax.div(to, GROUPS) + core, lax.rem(to, GROUPS)),
            device_id_type=MESH,
        ).start()

    y_own = pltpu.make_async_copy(y_send.at[spot], y_all.at[channel], own_sem.at[1])
    y_own.start()
    wait_bytes(h_send.at[pl.ds(0, 480)], h_out)
    wait_bytes(u_send.at[pl.ds(0, 480)], u_out)
    wait_bytes(h_all.at[pl.ds(0, 512)], twin_out.at[0])
    wait_bytes(u_all.at[pl.ds(0, 512)], twin_out.at[1])
    wait_bytes(q_send.at[pl.ds(0, 112)], q_out)
    wait_bytes(y_send.at[pl.ds(0, CHIPS * GROUPS - 1)], y_out)
    q_own.wait()
    y_own.wait()
    wait_bytes(q_all.at[pl.ds(0, 112)], q_arrived)
    wait_bytes(y_all.at[pl.ds(0, CHIPS * GROUPS - 1)], y_arrived)


def body(query_proj, key_proj, value_proj, filter_taps, skip_bias):
    any_space = pl.BlockSpec(memory_space=pl.ANY)
    dma = pltpu.SemaphoreType.DMA
    consts = [jnp.asarray(t) for t in tables()]
    y, q = pl.pallas_call(
        kernel,
        out_shape=[pltpu.VMEM((128, 4, 128), F32), pltpu.VMEM((128, 512), F32)],
        in_specs=[any_space] * 10,
        out_specs=[any_space] * 2,
        scratch_shapes=[
            pltpu.VMEM((16, 4096), BF16),
            pltpu.VMEM((16, 4096), BF16),
            pltpu.VMEM((16, 4096), BF16),
            pltpu.VMEM((16, 4096), F32),
            pltpu.VMEM((2, ROWS, ROWS), BF16),
            pltpu.VMEM((2, 2 * COLS, 2 * COLS), BF16),
            pltpu.VMEM((2, 2 * COLS, 2 * COLS), BF16),
            pltpu.VMEM((2, ROWS, ROWS), BF16),
            pltpu.VMEM((2, HALF, COLS), F32),
            pltpu.VMEM((512, 128), F32),
            pltpu.VMEM((512, 128), F32),
            pltpu.VMEM((1024, 128), F32),
            pltpu.VMEM((1024, 128), F32),
            pltpu.VMEM((128, 512), F32),
            pltpu.VMEM((128, 4, 128), F32),
            pltpu.VMEM((HALF, COLS), F32),
            pltpu.VMEM((HALF, COLS), F32),
            pltpu.SMEM((CHIPS,), F32),
            dma((10,)),
            dma,
            dma,
            dma((CHIPS,)),
            dma((CHIPS,)),
            dma((2,)),
            dma((2,)),
            dma,
            dma,
            dma,
            dma,
            dma,
            dma,
            pltpu.SemaphoreType.REGULAR,
            dma((2,)),
        ],
        compiler_params=pltpu.CompilerParams(
            collective_id=0, has_side_effects=True, vmem_limit_bytes=107 * 2**19
        ),
        cost_estimate=pl.CostEstimate(flops=2_400_000_000, bytes_accessed=6_000_000, transcendentals=0),
    )(query_proj, key_proj, value_proj, filter_taps, skip_bias, *consts)
    return y.reshape(128, 512) * q


def solution(mesh):
    placed = (P("chan", "seq"), P("chan", "seq"), P("chan", "seq"), P("chan", "seq"), P("chan"))
    return jax.shard_map(
        body, mesh=mesh, in_specs=placed, out_specs=P(None, ("seq", "chan")), check_vma=False
    )
```

```python
import math

import jax
import jax.numpy as jnp
import ml_dtypes
import numpy as np
from jax import lax
from jax.experimental import pallas as pl
from jax.experimental.pallas import tpu as pltpu
from jax.sharding import PartitionSpec as P

MESH = pl.DeviceIdType.MESH
F32 = jnp.float32
BF16 = jnp.bfloat16

ROWS = 512
COLS = 256
LENGTH = ROWS * COLS
CHIPS = 16
GROUPS = 8
HALF = ROWS // 2

TAPS_ORDER = [4 * z + y for z in (3, 2, 0, 1) for y in (3, 2, 1, 0) if z + y]
INPUT_ORDER = [4 * z + y for z in (1, 0, 3, 2) for y in (3, 2, 1, 0) if z + y]


def halves(table):
    high = table.astype(np.float32).astype(ml_dtypes.bfloat16)
    low = (table - high.astype(np.float64)).astype(np.float32).astype(ml_dtypes.bfloat16)
    return np.stack([high, low], axis=-3)


def tables():
    n1 = np.arange(ROWS, dtype=np.int64)
    n2 = np.arange(COLS, dtype=np.int64)
    angle = 2.0 * math.pi * (n2[:, None] * n2[None, :] % COLS) / COLS
    cos, sin = np.cos(angle), np.sin(angle)
    second = halves(np.block([[cos, -sin], [sin, cos]]))
    second_back = halves(np.block([[cos, sin], [-sin, cos]]))
    first, first_back, twiddle = [], [], []
    for core in range(2):
        k1 = core * HALF + np.arange(HALF, dtype=np.int64)
        angle = 2.0 * math.pi * (n1[None, :] * (4 * k1[:, None] + 1) % (4 * ROWS)) / (4 * ROWS)
        first.append(np.concatenate([np.cos(angle), -np.sin(angle)], axis=0))
        order = []
        for owner in (core, 1 - core):
            for bit in range(2):
                for chip in range(CHIPS):
                    for group in range(GROUPS):
                        order.append(((2 * chip + owner) * GROUPS + group) * 2 + bit)
        back = np.concatenate([np.cos(angle), -np.sin(angle)], axis=0).T / LENGTH
        first_back.append(back[np.array(order)])
        angle = 2.0 * math.pi * (n2[None, :] * (4 * k1[:, None] + 1) % (4 * LENGTH)) / (4 * LENGTH)
        twiddle.append(np.stack([np.cos(angle), -np.sin(angle)]))
    return (
        halves(np.stack(first)),
        second,
        second_back,
        halves(np.stack(first_back)),
        np.stack(twiddle).astype(np.float32),
    )


def split(value):
    high = value.astype(BF16)
    low = (value - high.astype(F32)).astype(BF16)
    return high, low


def dot3(left, right):
    def one(a, b):
        return jnp.dot(a, b, preferred_element_type=F32)

    return one(left[0], right[0]) + (one(left[0], right[1]) + one(left[1], right[0]))


def kernel(
    q_ref, k_ref, v_ref, h_ref, b_ref, f1_ref, f2_ref, g2_ref, g1_ref, tw_ref, y_all, q_all,
    q_in, k_in, v_in, h_in, f1, f2, g2, g1, tw,
    h_send, u_send, h_all, u_all, q_send, y_send, part_send, part_all,
    bias_ref, in_sem, h_out, u_out, h_arrived, u_arrived, twin_out, twin_arrived,
    q_out, q_arrived, part_out, part_arrived, y_out, y_arrived, ready, own_sem,
):
    s = lax.axis_index("seq")
    g = lax.axis_index("chan")
    core = lax.rem(s, 2)
    chip = lax.div(s, 2)
    twin = s + 1 - 2 * core

    pairs = [
        (h_ref, h_in),
        (k_ref, k_in),
        (v_ref, v_in),
        (q_ref, q_in),
        (f1_ref.at[core], f1),
        (tw_ref.at[core], tw),
        (f2_ref, f2),
        (g2_ref, g2),
        (g1_ref.at[core], g1),
        (b_ref, bias_ref),
    ]
    loads = [pltpu.make_async_copy(a, b, in_sem.at[n]) for n, (a, b) in enumerate(pairs)]
    loads[0].start()
    loads[9].start()

    barrier = pltpu.get_barrier_semaphore()

    @pl.loop(1, CHIPS)
    def _(d):
        pl.semaphore_signal(barrier, inc=1, device_id=(2 * lax.rem(chip + d, CHIPS) + core, g), device_id_type=MESH)

    pl.semaphore_signal(barrier, inc=1, device_id=(twin, g), device_id_type=MESH)

    @pl.loop(1, GROUPS)
    def _(d):
        pl.semaphore_signal(barrier, inc=1, device_id=(s, lax.rem(g + d, GROUPS)), device_id_type=MESH)

    for load in loads[1:9]:
        load.start()

    loads[0].wait()
    loads[9].wait()
    row = lax.broadcasted_iota(jnp.int32, (CHIPS, 128), 0)
    lane = lax.broadcasted_iota(jnp.int32, (CHIPS, 128), 1)
    direct = jnp.zeros((CHIPS, 128), F32)
    for c in range(CHIPS):
        direct = jnp.where(row == c, bias_ref[c], direct)
    direct = jnp.where((lane == 0) & (s == 0), direct, 0.0)
    h_in[:, 0:128] = h_in[:, 0:128] + direct
    for j in range(32):
        h_send[pl.ds(16 * (j % 2) + j // 2, CHIPS, stride=32), :] = h_in[:, 128 * j : 128 * j + 128]
    pl.semaphore_wait(barrier, CHIPS + GROUPS - 1)

    def outward(src, dst, out_sem, arrived, order):
        for d in order:
            to = chip ^ d
            pltpu.make_async_remote_copy(
                src_ref=src.at[pl.ds(pl.multiple_of(32 * to, 32), 32)],
                dst_ref=dst.at[pl.ds(pl.multiple_of(32 * s, 32), 32)],
                send_sem=out_sem,
                recv_sem=arrived.at[chip],
                device_id=(2 * to + core, g),
                device_id_type=MESH,
            ).start()

    def to_twin(array, n):
        rows = array.at[pl.ds(pl.multiple_of(32 * (2 * n + core), 32), 32)]
        return rows

    def own(src, dst, sem, arrived):
        dst[pl.ds(pl.multiple_of(32 * s, 32), 32)] = src[pl.ds(pl.multiple_of(32 * chip, 32), 32)]
        rows = to_twin(dst, chip)
        pltpu.make_async_remote_copy(
            src_ref=rows, dst_ref=rows, send_sem=sem, recv_sem=arrived, device_id=(twin, g), device_id_type=MESH
        ).start()

    def pass_on(array, arrived, n, order):
        for d in order:
            source = chip ^ d
            rows = to_twin(array, source)
            pltpu.make_async_copy(rows, rows, arrived.at[source]).wait()
            pltpu.make_async_remote_copy(
                src_ref=rows,
                dst_ref=rows,
                send_sem=twin_out.at[n],
                recv_sem=twin_arrived.at[n],
                device_id=(twin, g),
                device_id_type=MESH,
            ).start()

    def wait_bytes(array, sem):
        pltpu.make_async_copy(array, array, sem).wait()

    outward(h_send, h_all, h_out, h_arrived, TAPS_ORDER)

    @pl.loop(1, GROUPS)
    def _(d):
        pl.semaphore_signal(ready, inc=1, device_id=(s, lax.rem(g + d, GROUPS)), device_id_type=MESH)

    own(h_send, h_all, twin_out.at[0], twin_arrived.at[0])

    loads[1].wait()
    loads[2].wait()
    for j in range(32):
        cols = slice(128 * j, 128 * j + 128)
        u_send[pl.ds(16 * (j % 2) + j // 2, CHIPS, stride=32), :] = k_in[:, cols].astype(F32) * v_in[:, cols].astype(F32)
    outward(u_send, u_all, u_out, u_arrived, INPUT_ORDER)
    own(u_send, u_all, twin_out.at[1], twin_arrived.at[1])

    loads[3].wait()
    for j in range(GROUPS):
        q_send[16 * j : 16 * j + 16, :] = q_in[:, 512 * j : 512 * j + 512].astype(F32)

    def send_query(z_half, first):
        @pl.loop(first, GROUPS // 2)
        def _(d):
            to = 2 * lax.rem(lax.div(g, 2) + d, GROUPS // 2) + z_half
            pltpu.make_async_remote_copy(
                src_ref=q_send.at[pl.ds(pl.multiple_of(16 * to, 16), 16)],
                dst_ref=q_all.at[pl.ds(pl.multiple_of(16 * g, 16), 16)],
                send_sem=q_out,
                recv_sem=q_arrived,
                device_id=(s, to),
                device_id_type=MESH,
            ).start()

    q_rows = pl.ds(pl.multiple_of(16 * g, 16), 16)
    q_own = pltpu.make_async_copy(q_send.at[q_rows], q_all.at[q_rows], own_sem.at[0])
    q_own.start()
    send_query(lax.rem(g, 2), 1)

    for n in range(4, 9):
        loads[n].wait()

    def forward(array):
        halves_of = [
            jnp.concatenate([array[32 * n + 16 * odd : 32 * n + 16 * odd + 16, :] for n in range(2 * CHIPS)], axis=0)
            for odd in range(2)
        ]
        points = jnp.concatenate(halves_of, axis=1)
        a = dot3((f1[0], f1[1]), split(points))
        re, im = a[:HALF], a[HALF:]
        b = jnp.concatenate([re * tw[0] - im * tw[1], re * tw[1] + im * tw[0]], axis=1)
        return dot3(split(b), (f2[0], f2[1]))

    pass_on(h_all, h_arrived, 0, TAPS_ORDER)
    wait_bytes(h_all.at[pl.ds(0, 512)], twin_arrived.at[0])
    hf = forward(h_all)

    pass_on(u_all, u_arrived, 1, INPUT_ORDER[:-2])
    send_query(1 - lax.rem(g, 2), 0)
    pass_on(u_all, u_arrived, 1, INPUT_ORDER[-2:])

    wait_bytes(u_all.at[pl.ds(0, 512)], twin_arrived.at[1])
    uf = forward(u_all)
    ur, ui, hr, hi = uf[:, :COLS], uf[:, COLS:], hf[:, :COLS], hf[:, COLS:]
    y = jnp.concatenate([ur * hr - ui * hi, ur * hi + ui * hr], axis=1)
    b = dot3(split(y), (g2[0], g2[1]))
    re, im = b[:, :COLS], b[:, COLS:]
    e = split(jnp.concatenate([re * tw[0] + im * tw[1], im * tw[0] - re * tw[1]], axis=0))
    part_send[...] = dot3((g1[0, HALF:], g1[1, HALF:]), e)
    exchange = pltpu.make_async_remote_copy(
        src_ref=part_send,
        dst_ref=part_all,
        send_sem=part_out,
        recv_sem=part_arrived,
        device_id=(twin, g),
        device_id_type=MESH,
    )
    exchange.start()
    mine = dot3((g1[0, :HALF], g1[1, :HALF]), e)
    exchange.wait()
    mine = mine + part_all[...]
    for bit in range(2):
        for side in range(2):
            y_send[:, 2 * bit + side, :] = mine[128 * bit : 128 * bit + 128, 128 * side : 128 * side + 128]

    spot = chip * GROUPS + g
    channel = g * CHIPS + chip

    pl.semaphore_wait(ready, GROUPS - 1)

    @pl.loop(1, CHIPS * GROUPS, unroll=4)
    def _(d):
        to = lax.rem(spot + d, CHIPS * GROUPS)
        pltpu.make_async_remote_copy(
            src_ref=y_send.at[to],
            dst_ref=y_all.at[channel],
            send_sem=y_out,
            recv_sem=y_arrived,
            device_id=(2 * lax.div(to, GROUPS) + core, lax.rem(to, GROUPS)),
            device_id_type=MESH,
        ).start()

    y_own = pltpu.make_async_copy(y_send.at[spot], y_all.at[channel], own_sem.at[1])
    y_own.start()
    wait_bytes(h_send.at[pl.ds(0, 480)], h_out)
    wait_bytes(u_send.at[pl.ds(0, 480)], u_out)
    wait_bytes(h_all.at[pl.ds(0, 512)], twin_out.at[0])
    wait_bytes(u_all.at[pl.ds(0, 512)], twin_out.at[1])
    wait_bytes(q_send.at[pl.ds(0, 112)], q_out)
    wait_bytes(y_send.at[pl.ds(0, CHIPS * GROUPS - 1)], y_out)
    q_own.wait()
    y_own.wait()
    wait_bytes(q_all.at[pl.ds(0, 112)], q_arrived)
    wait_bytes(y_all.at[pl.ds(0, CHIPS * GROUPS - 1)], y_arrived)


def body(query_proj, key_proj, value_proj, filter_taps, skip_bias):
    any_space = pl.BlockSpec(memory_space=pl.ANY)
    dma = pltpu.SemaphoreType.DMA
    consts = [jnp.asarray(t) for t in tables()]
    y, q = pl.pallas_call(
        kernel,
        out_shape=[pltpu.VMEM((128, 4, 128), F32), pltpu.VMEM((128, 512), F32)],
        in_specs=[any_space] * 10,
        out_specs=[any_space] * 2,
        scratch_shapes=[
            pltpu.VMEM((16, 4096), BF16),
            pltpu.VMEM((16, 4096), BF16),
            pltpu.VMEM((16, 4096), BF16),
            pltpu.VMEM((16, 4096), F32),
            pltpu.VMEM((2, ROWS, ROWS), BF16),
            pltpu.VMEM((2, 2 * COLS, 2 * COLS), BF16),
            pltpu.VMEM((2, 2 * COLS, 2 * COLS), BF16),
            pltpu.VMEM((2, ROWS, ROWS), BF16),
            pltpu.VMEM((2, HALF, COLS), F32),
            pltpu.VMEM((512, 128), F32),
            pltpu.VMEM((512, 128), F32),
            pltpu.VMEM((1024, 128), F32),
            pltpu.VMEM((1024, 128), F32),
            pltpu.VMEM((128, 512), F32),
            pltpu.VMEM((128, 4, 128), F32),
            pltpu.VMEM((HALF, COLS), F32),
            pltpu.VMEM((HALF, COLS), F32),
            pltpu.SMEM((CHIPS,), F32),
            dma((10,)),
            dma,
            dma,
            dma((CHIPS,)),
            dma((CHIPS,)),
            dma((2,)),
            dma((2,)),
            dma,
            dma,
            dma,
            dma,
            dma,
            dma,
            pltpu.SemaphoreType.REGULAR,
            dma((2,)),
        ],
        compiler_params=pltpu.CompilerParams(
            collective_id=0, has_side_effects=True, vmem_limit_bytes=107 * 2**19
        ),
        cost_estimate=pl.CostEstimate(flops=2_400_000_000, bytes_accessed=6_000_000, transcendentals=0),
    )(query_proj, key_proj, value_proj, filter_taps, skip_bias, *consts)
    return y.reshape(128, 512) * q


def solution(mesh):
    placed = (P("chan", "seq"), P("chan", "seq"), P("chan", "seq"), P("chan", "seq"), P("chan"))
    return jax.shard_map(
        body, mesh=mesh, in_specs=placed, out_specs=P(None, ("seq", "chan")), check_vma=False
    )
```

```python
import math

import jax
import jax.numpy as jnp
import ml_dtypes
import numpy as np
from jax import lax
from jax.experimental import pallas as pl
from jax.experimental.pallas import tpu as pltpu
from jax.sharding import PartitionSpec as P

MESH = pl.DeviceIdType.MESH
F32 = jnp.float32
BF16 = jnp.bfloat16

ROWS = 512
COLS = 256
LENGTH = ROWS * COLS
CHIPS = 16
GROUPS = 8
HALF = ROWS // 2

TAPS_ORDER = [4 * z + y for z in (3, 2, 0, 1) for y in (3, 2, 1, 0) if z + y]
INPUT_ORDER = [4 * z + y for z in (1, 0, 3, 2) for y in (3, 2, 1, 0) if z + y]


def halves(table):
    high = table.astype(np.float32).astype(ml_dtypes.bfloat16)
    low = (table - high.astype(np.float64)).astype(np.float32).astype(ml_dtypes.bfloat16)
    return np.stack([high, low], axis=-3)


def tables():
    n1 = np.arange(ROWS, dtype=np.int64)
    n2 = np.arange(COLS, dtype=np.int64)
    angle = 2.0 * math.pi * (n2[:, None] * n2[None, :] % COLS) / COLS
    cos, sin = np.cos(angle), np.sin(angle)
    second = halves(np.block([[cos, -sin], [sin, cos]]))
    second_back = halves(np.block([[cos, sin], [-sin, cos]]))
    first, first_back, twiddle = [], [], []
    for core in range(2):
        k1 = core * HALF + np.arange(HALF, dtype=np.int64)
        angle = 2.0 * math.pi * (n1[None, :] * (4 * k1[:, None] + 1) % (4 * ROWS)) / (4 * ROWS)
        first.append(np.concatenate([np.cos(angle), -np.sin(angle)], axis=0))
        order = []
        for owner in (core, 1 - core):
            for bit in range(2):
                for chip in range(CHIPS):
                    for group in range(GROUPS):
                        order.append(((2 * chip + owner) * GROUPS + group) * 2 + bit)
        back = np.concatenate([np.cos(angle), -np.sin(angle)], axis=0).T / LENGTH
        first_back.append(back[np.array(order)])
        angle = 2.0 * math.pi * (n2[None, :] * (4 * k1[:, None] + 1) % (4 * LENGTH)) / (4 * LENGTH)
        twiddle.append(np.stack([np.cos(angle), -np.sin(angle)]))
    return (
        halves(np.stack(first)),
        second,
        second_back,
        halves(np.stack(first_back)),
        np.stack(twiddle).astype(np.float32),
    )


def split(value):
    high = value.astype(BF16)
    low = (value - high.astype(F32)).astype(BF16)
    return high, low


def dot3(left, right):
    def one(a, b):
        return jnp.dot(a, b, preferred_element_type=F32)

    return one(left[0], right[0]) + (one(left[0], right[1]) + one(left[1], right[0]))


def kernel(
    q_ref, k_ref, v_ref, h_ref, b_ref, f1_ref, f2_ref, g2_ref, g1_ref, tw_ref, y_all, q_all,
    q_in, k_in, v_in, h_in, f1, f2, g2, g1, tw,
    h_send, u_send, h_all, u_all, q_send, y_send, part_send, part_all,
    bias_ref, in_sem, h_out, u_out, h_arrived, u_arrived, twin_out, twin_arrived,
    q_out, q_arrived, part_out, part_arrived, y_out, y_arrived, ready, own_sem,
):
    s = lax.axis_index("seq")
    g = lax.axis_index("chan")
    core = lax.rem(s, 2)
    chip = lax.div(s, 2)
    twin = s + 1 - 2 * core

    pairs = [
        (h_ref, h_in),
        (k_ref, k_in),
        (v_ref, v_in),
        (q_ref, q_in),
        (f1_ref.at[core], f1),
        (tw_ref.at[core], tw),
        (f2_ref, f2),
        (g2_ref, g2),
        (g1_ref.at[core], g1),
        (b_ref, bias_ref),
    ]
    loads = [pltpu.make_async_copy(a, b, in_sem.at[n]) for n, (a, b) in enumerate(pairs)]
    loads[0].start()
    loads[9].start()

    barrier = pltpu.get_barrier_semaphore()

    @pl.loop(1, CHIPS)
    def _(d):
        pl.semaphore_signal(barrier, inc=1, device_id=(2 * lax.rem(chip + d, CHIPS) + core, g), device_id_type=MESH)

    pl.semaphore_signal(barrier, inc=1, device_id=(twin, g), device_id_type=MESH)

    @pl.loop(1, GROUPS)
    def _(d):
        pl.semaphore_signal(barrier, inc=1, device_id=(s, lax.rem(g + d, GROUPS)), device_id_type=MESH)

    for load in loads[1:9]:
        load.start()

    loads[0].wait()
    loads[9].wait()
    row = lax.broadcasted_iota(jnp.int32, (CHIPS, 128), 0)
    lane = lax.broadcasted_iota(jnp.int32, (CHIPS, 128), 1)
    direct = jnp.zeros((CHIPS, 128), F32)
    for c in range(CHIPS):
        direct = jnp.where(row == c, bias_ref[c], direct)
    direct = jnp.where((lane == 0) & (s == 0), direct, 0.0)
    h_in[:, 0:128] = h_in[:, 0:128] + direct
    for j in range(32):
        h_send[pl.ds(16 * (j % 2) + j // 2, CHIPS, stride=32), :] = h_in[:, 128 * j : 128 * j + 128]
    pl.semaphore_wait(barrier, CHIPS + GROUPS - 1)

    def outward(src, dst, out_sem, arrived, order):
        for d in order:
            to = chip ^ d
            pltpu.make_async_remote_copy(
                src_ref=src.at[pl.ds(pl.multiple_of(32 * to, 32), 32)],
                dst_ref=dst.at[pl.ds(pl.multiple_of(32 * s, 32), 32)],
                send_sem=out_sem,
                recv_sem=arrived.at[chip],
                device_id=(2 * to + core, g),
                device_id_type=MESH,
            ).start()

    def to_twin(array, n):
        rows = array.at[pl.ds(pl.multiple_of(32 * (2 * n + core), 32), 32)]
        return rows

    def own(src, dst, sem, arrived):
        dst[pl.ds(pl.multiple_of(32 * s, 32), 32)] = src[pl.ds(pl.multiple_of(32 * chip, 32), 32)]
        rows = to_twin(dst, chip)
        pltpu.make_async_remote_copy(
            src_ref=rows, dst_ref=rows, send_sem=sem, recv_sem=arrived, device_id=(twin, g), device_id_type=MESH
        ).start()

    def pass_on(array, arrived, n, order):
        for d in order:
            source = chip ^ d
            rows = to_twin(array, source)
            pltpu.make_async_copy(rows, rows, arrived.at[source]).wait()
            pltpu.make_async_remote_copy(
                src_ref=rows,
                dst_ref=rows,
                send_sem=twin_out.at[n],
                recv_sem=twin_arrived.at[n],
                device_id=(twin, g),
                device_id_type=MESH,
            ).start()

    def wait_bytes(array, sem):
        pltpu.make_async_copy(array, array, sem).wait()

    outward(h_send, h_all, h_out, h_arrived, TAPS_ORDER)

    @pl.loop(1, GROUPS)
    def _(d):
        pl.semaphore_signal(ready, inc=1, device_id=(s, lax.rem(g + d, GROUPS)), device_id_type=MESH)

    own(h_send, h_all, twin_out.at[0], twin_arrived.at[0])

    loads[1].wait()
    loads[2].wait()
    for j in range(32):
        cols = slice(128 * j, 128 * j + 128)
        u_send[pl.ds(16 * (j % 2) + j // 2, CHIPS, stride=32), :] = k_in[:, cols].astype(F32) * v_in[:, cols].astype(F32)
    outward(u_send, u_all, u_out, u_arrived, INPUT_ORDER)
    own(u_send, u_all, twin_out.at[1], twin_arrived.at[1])

    loads[3].wait()
    for j in range(GROUPS):
        q_send[16 * j : 16 * j + 16, :] = q_in[:, 512 * j : 512 * j + 512].astype(F32)

    def send_query(z_half, first):
        @pl.loop(first, GROUPS // 2)
        def _(d):
            to = 2 * lax.rem(lax.div(g, 2) + d, GROUPS // 2) + z_half
            pltpu.make_async_remote_copy(
                src_ref=q_send.at[pl.ds(pl.multiple_of(16 * to, 16), 16)],
                dst_ref=q_all.at[pl.ds(pl.multiple_of(16 * g, 16), 16)],
                send_sem=q_out,
                recv_sem=q_arrived,
                device_id=(s, to),
                device_id_type=MESH,
            ).start()

    q_rows = pl.ds(pl.multiple_of(16 * g, 16), 16)
    q_own = pltpu.make_async_copy(q_send.at[q_rows], q_all.at[q_rows], own_sem.at[0])
    q_own.start()
    send_query(lax.rem(g, 2), 1)

    for n in range(4, 9):
        loads[n].wait()

    def forward(array):
        halves_of = [
            jnp.concatenate([array[32 * n + 16 * odd : 32 * n + 16 * odd + 16, :] for n in range(2 * CHIPS)], axis=0)
            for odd in range(2)
        ]
        points = jnp.concatenate(halves_of, axis=1)
        a = dot3((f1[0], f1[1]), split(points))
        re, im = a[:HALF], a[HALF:]
        b = jnp.concatenate([re * tw[0] - im * tw[1], re * tw[1] + im * tw[0]], axis=1)
        return dot3(split(b), (f2[0], f2[1]))

    pass_on(h_all, h_arrived, 0, TAPS_ORDER)
    wait_bytes(h_all.at[pl.ds(0, 512)], twin_arrived.at[0])
    hf = forward(h_all)

    pass_on(u_all, u_arrived, 1, INPUT_ORDER[:-2])
    send_query(1 - lax.rem(g, 2), 0)
    pass_on(u_all, u_arrived, 1, INPUT_ORDER[-2:])

    wait_bytes(u_all.at[pl.ds(0, 512)], twin_arrived.at[1])
    uf = forward(u_all)
    ur, ui, hr, hi = uf[:, :COLS], uf[:, COLS:], hf[:, :COLS], hf[:, COLS:]
    y = jnp.concatenate([ur * hr - ui * hi, ur * hi + ui * hr], axis=1)
    b = dot3(split(y), (g2[0], g2[1]))
    re, im = b[:, :COLS], b[:, COLS:]
    e = split(jnp.concatenate([re * tw[0] + im * tw[1], im * tw[0] - re * tw[1]], axis=0))
    part_send[...] = dot3((g1[0, HALF:], g1[1, HALF:]), e)
    exchange = pltpu.make_async_remote_copy(
        src_ref=part_send,
        dst_ref=part_all,
        send_sem=part_out,
        recv_sem=part_arrived,
        device_id=(twin, g),
        device_id_type=MESH,
    )
    exchange.start()
    mine = dot3((g1[0, :HALF], g1[1, :HALF]), e)
    exchange.wait()
    mine = mine + part_all[...]
    for bit in range(2):
        for side in range(2):
            y_send[:, 2 * bit + side, :] = mine[128 * bit : 128 * bit + 128, 128 * side : 128 * side + 128]

    spot = chip * GROUPS + g
    channel = g * CHIPS + chip

    pl.semaphore_wait(ready, GROUPS - 1)

    @pl.loop(1, CHIPS * GROUPS, unroll=4)
    def _(d):
        step = jnp.where(d <= 64, 2 * d - 1, 2 * (d - 64))
        to = lax.rem(spot + step, CHIPS * GROUPS)
        pltpu.make_async_remote_copy(
            src_ref=y_send.at[to],
            dst_ref=y_all.at[channel],
            send_sem=y_out,
            recv_sem=y_arrived,
            device_id=(2 * lax.div(to, GROUPS) + core, lax.rem(to, GROUPS)),
            device_id_type=MESH,
        ).start()

    y_own = pltpu.make_async_copy(y_send.at[spot], y_all.at[channel], own_sem.at[1])
    y_own.start()
    wait_bytes(h_send.at[pl.ds(0, 480)], h_out)
    wait_bytes(u_send.at[pl.ds(0, 480)], u_out)
    wait_bytes(h_all.at[pl.ds(0, 512)], twin_out.at[0])
    wait_bytes(u_all.at[pl.ds(0, 512)], twin_out.at[1])
    wait_bytes(q_send.at[pl.ds(0, 112)], q_out)
    wait_bytes(y_send.at[pl.ds(0, CHIPS * GROUPS - 1)], y_out)
    q_own.wait()
    y_own.wait()
    wait_bytes(q_all.at[pl.ds(0, 112)], q_arrived)
    wait_bytes(y_all.at[pl.ds(0, CHIPS * GROUPS - 1)], y_arrived)


def body(query_proj, key_proj, value_proj, filter_taps, skip_bias):
    any_space = pl.BlockSpec(memory_space=pl.ANY)
    dma = pltpu.SemaphoreType.DMA
    consts = [jnp.asarray(t) for t in tables()]
    y, q = pl.pallas_call(
        kernel,
        out_shape=[pltpu.VMEM((128, 4, 128), F32), pltpu.VMEM((128, 512), F32)],
        in_specs=[any_space] * 10,
        out_specs=[any_space] * 2,
        scratch_shapes=[
            pltpu.VMEM((16, 4096), BF16),
            pltpu.VMEM((16, 4096), BF16),
            pltpu.VMEM((16, 4096), BF16),
            pltpu.VMEM((16, 4096), F32),
            pltpu.VMEM((2, ROWS, ROWS), BF16),
            pltpu.VMEM((2, 2 * COLS, 2 * COLS), BF16),
            pltpu.VMEM((2, 2 * COLS, 2 * COLS), BF16),
            pltpu.VMEM((2, ROWS, ROWS), BF16),
            pltpu.VMEM((2, HALF, COLS), F32),
            pltpu.VMEM((512, 128), F32),
            pltpu.VMEM((512, 128), F32),
            pltpu.VMEM((1024, 128), F32),
            pltpu.VMEM((1024, 128), F32),
            pltpu.VMEM((128, 512), F32),
            pltpu.VMEM((128, 4, 128), F32),
            pltpu.VMEM((HALF, COLS), F32),
            pltpu.VMEM((HALF, COLS), F32),
            pltpu.SMEM((CHIPS,), F32),
            dma((10,)),
            dma,
            dma,
            dma((CHIPS,)),
            dma((CHIPS,)),
            dma((2,)),
            dma((2,)),
            dma,
            dma,
            dma,
            dma,
            dma,
            dma,
            pltpu.SemaphoreType.REGULAR,
            dma((2,)),
        ],
        compiler_params=pltpu.CompilerParams(
            collective_id=0, has_side_effects=True, vmem_limit_bytes=107 * 2**19
        ),
        cost_estimate=pl.CostEstimate(flops=2_400_000_000, bytes_accessed=6_000_000, transcendentals=0),
    )(query_proj, key_proj, value_proj, filter_taps, skip_bias, *consts)
    return y.reshape(128, 512) * q


def solution(mesh):
    placed = (P("chan", "seq"), P("chan", "seq"), P("chan", "seq"), P("chan", "seq"), P("chan"))
    return jax.shard_map(
        body, mesh=mesh, in_specs=placed, out_specs=P(None, ("seq", "chan")), check_vma=False
    )
```

```python
import math

import jax
import jax.numpy as jnp
import ml_dtypes
import numpy as np
from jax import lax
from jax.experimental import pallas as pl
from jax.experimental.pallas import tpu as pltpu
from jax.sharding import PartitionSpec as P

MESH = pl.DeviceIdType.MESH
F32 = jnp.float32
BF16 = jnp.bfloat16

ROWS = 512
COLS = 256
LENGTH = ROWS * COLS
CHIPS = 16
GROUPS = 8
HALF = ROWS // 2

TAPS_ORDER = [4 * z + y for z in (3, 2, 0, 1) for y in (3, 2, 1, 0) if z + y]
INPUT_ORDER = [4 * z + y for z in (1, 0, 3, 2) for y in (3, 2, 1, 0) if z + y]


def halves(table):
    high = table.astype(np.float32).astype(ml_dtypes.bfloat16)
    low = (table - high.astype(np.float64)).astype(np.float32).astype(ml_dtypes.bfloat16)
    return np.stack([high, low], axis=-3)


def tables():
    n1 = np.arange(ROWS, dtype=np.int64)
    n2 = np.arange(COLS, dtype=np.int64)
    angle = 2.0 * math.pi * (n2[:, None] * n2[None, :] % COLS) / COLS
    cos, sin = np.cos(angle), np.sin(angle)
    second = halves(np.block([[cos, -sin], [sin, cos]]))
    second_back = halves(np.block([[cos, sin], [-sin, cos]]))
    first, first_back, twiddle = [], [], []
    for core in range(2):
        k1 = core * HALF + np.arange(HALF, dtype=np.int64)
        angle = 2.0 * math.pi * (n1[None, :] * (4 * k1[:, None] + 1) % (4 * ROWS)) / (4 * ROWS)
        first.append(np.concatenate([np.cos(angle), -np.sin(angle)], axis=0))
        order = []
        for owner in (core, 1 - core):
            for bit in range(2):
                for chip in range(CHIPS):
                    for group in range(GROUPS):
                        order.append(((2 * chip + owner) * GROUPS + group) * 2 + bit)
        back = np.concatenate([np.cos(angle), -np.sin(angle)], axis=0).T / LENGTH
        first_back.append(back[np.array(order)])
        angle = 2.0 * math.pi * (n2[None, :] * (4 * k1[:, None] + 1) % (4 * LENGTH)) / (4 * LENGTH)
        twiddle.append(np.stack([np.cos(angle), -np.sin(angle)]))
    return (
        halves(np.stack(first)),
        second,
        second_back,
        halves(np.stack(first_back)),
        np.stack(twiddle).astype(np.float32),
    )


def split(value):
    high = value.astype(BF16)
    low = (value - high.astype(F32)).astype(BF16)
    return high, low


def dot3(left, right):
    def one(a, b):
        return jnp.dot(a, b, preferred_element_type=F32)

    return one(left[0], right[0]) + (one(left[0], right[1]) + one(left[1], right[0]))


def kernel(
    q_ref, k_ref, v_ref, h_ref, b_ref, f1_ref, f2_ref, g2_ref, g1_ref, tw_ref, y_all, q_all,
    q_in, k_in, v_in, h_in, f1, f2, g2, g1, tw,
    h_send, u_send, h_all, u_all, q_send, y_send, part_send, part_all,
    bias_ref, in_sem, h_out, u_out, h_arrived, u_arrived, twin_out, twin_arrived,
    q_out, q_arrived, part_out, part_arrived, y_out, y_arrived, ready, own_sem,
):
    s = lax.axis_index("seq")
    g = lax.axis_index("chan")
    core = lax.rem(s, 2)
    chip = lax.div(s, 2)
    twin = s + 1 - 2 * core

    pairs = [
        (h_ref, h_in),
        (k_ref, k_in),
        (v_ref, v_in),
        (q_ref, q_in),
        (f1_ref.at[core], f1),
        (tw_ref.at[core], tw),
        (f2_ref, f2),
        (g2_ref, g2),
        (g1_ref.at[core], g1),
        (b_ref, bias_ref),
    ]
    loads = [pltpu.make_async_copy(a, b, in_sem.at[n]) for n, (a, b) in enumerate(pairs)]
    loads[0].start()
    loads[9].start()

    barrier = pltpu.get_barrier_semaphore()

    @pl.loop(1, CHIPS)
    def _(d):
        pl.semaphore_signal(barrier, inc=1, device_id=(2 * lax.rem(chip + d, CHIPS) + core, g), device_id_type=MESH)

    pl.semaphore_signal(barrier, inc=1, device_id=(twin, g), device_id_type=MESH)

    @pl.loop(1, GROUPS)
    def _(d):
        pl.semaphore_signal(barrier, inc=1, device_id=(s, lax.rem(g + d, GROUPS)), device_id_type=MESH)

    for load in loads[1:9]:
        load.start()

    loads[0].wait()
    loads[9].wait()
    row = lax.broadcasted_iota(jnp.int32, (CHIPS, 128), 0)
    lane = lax.broadcasted_iota(jnp.int32, (CHIPS, 128), 1)
    direct = jnp.zeros((CHIPS, 128), F32)
    for c in range(CHIPS):
        direct = jnp.where(row == c, bias_ref[c], direct)
    direct = jnp.where((lane == 0) & (s == 0), direct, 0.0)
    h_in[:, 0:128] = h_in[:, 0:128] + direct
    for j in range(32):
        h_send[pl.ds(16 * (j % 2) + j // 2, CHIPS, stride=32), :] = h_in[:, 128 * j : 128 * j + 128]
    pl.semaphore_wait(barrier, CHIPS + GROUPS - 1)

    def outward(src, dst, out_sem, arrived, order):
        for d in order:
            to = chip ^ d
            pltpu.make_async_remote_copy(
                src_ref=src.at[pl.ds(pl.multiple_of(32 * to, 32), 32)],
                dst_ref=dst.at[pl.ds(pl.multiple_of(32 * s, 32), 32)],
                send_sem=out_sem,
                recv_sem=arrived.at[chip],
                device_id=(2 * to + core, g),
                device_id_type=MESH,
            ).start()

    def to_twin(array, n):
        rows = array.at[pl.ds(pl.multiple_of(32 * (2 * n + core), 32), 32)]
        return rows

    def own(src, dst, sem, arrived):
        dst[pl.ds(pl.multiple_of(32 * s, 32), 32)] = src[pl.ds(pl.multiple_of(32 * chip, 32), 32)]
        rows = to_twin(dst, chip)
        pltpu.make_async_remote_copy(
            src_ref=rows, dst_ref=rows, send_sem=sem, recv_sem=arrived, device_id=(twin, g), device_id_type=MESH
        ).start()

    def pass_on(array, arrived, n, order):
        for d in order:
            source = chip ^ d
            rows = to_twin(array, source)
            pltpu.make_async_copy(rows, rows, arrived.at[source]).wait()
            pltpu.make_async_remote_copy(
                src_ref=rows,
                dst_ref=rows,
                send_sem=twin_out.at[n],
                recv_sem=twin_arrived.at[n],
                device_id=(twin, g),
                device_id_type=MESH,
            ).start()

    def wait_bytes(array, sem):
        pltpu.make_async_copy(array, array, sem).wait()

    outward(h_send, h_all, h_out, h_arrived, TAPS_ORDER)

    @pl.loop(1, GROUPS)
    def _(d):
        pl.semaphore_signal(ready, inc=1, device_id=(s, lax.rem(g + d, GROUPS)), device_id_type=MESH)

    own(h_send, h_all, twin_out.at[0], twin_arrived.at[0])

    loads[1].wait()
    loads[2].wait()
    for j in range(32):
        cols = slice(128 * j, 128 * j + 128)
        u_send[pl.ds(16 * (j % 2) + j // 2, CHIPS, stride=32), :] = k_in[:, cols].astype(F32) * v_in[:, cols].astype(F32)
    outward(u_send, u_all, u_out, u_arrived, INPUT_ORDER)
    own(u_send, u_all, twin_out.at[1], twin_arrived.at[1])

    loads[3].wait()
    for j in range(GROUPS):
        q_send[16 * j : 16 * j + 16, :] = q_in[:, 512 * j : 512 * j + 512].astype(F32)

    def send_query(z_half, first):
        @pl.loop(first, GROUPS // 2)
        def _(d):
            to = 2 * lax.rem(lax.div(g, 2) + d, GROUPS // 2) + z_half
            pltpu.make_async_remote_copy(
                src_ref=q_send.at[pl.ds(pl.multiple_of(16 * to, 16), 16)],
                dst_ref=q_all.at[pl.ds(pl.multiple_of(16 * g, 16), 16)],
                send_sem=q_out,
                recv_sem=q_arrived,
                device_id=(s, to),
                device_id_type=MESH,
            ).start()

    q_rows = pl.ds(pl.multiple_of(16 * g, 16), 16)
    q_own = pltpu.make_async_copy(q_send.at[q_rows], q_all.at[q_rows], own_sem.at[0])
    q_own.start()
    send_query(lax.rem(g, 2), 1)

    for n in range(4, 9):
        loads[n].wait()

    def forward(array):
        halves_of = [
            jnp.concatenate([array[32 * n + 16 * odd : 32 * n + 16 * odd + 16, :] for n in range(2 * CHIPS)], axis=0)
            for odd in range(2)
        ]
        points = jnp.concatenate(halves_of, axis=1)
        a = dot3((f1[0], f1[1]), split(points))
        re, im = a[:HALF], a[HALF:]
        b = jnp.concatenate([re * tw[0] - im * tw[1], re * tw[1] + im * tw[0]], axis=1)
        return dot3(split(b), (f2[0], f2[1]))

    pass_on(h_all, h_arrived, 0, TAPS_ORDER)
    wait_bytes(h_all.at[pl.ds(0, 512)], twin_arrived.at[0])
    hf = forward(h_all)

    pass_on(u_all, u_arrived, 1, INPUT_ORDER[:-4])
    send_query(1 - lax.rem(g, 2), 0)
    pass_on(u_all, u_arrived, 1, INPUT_ORDER[-4:])

    wait_bytes(u_all.at[pl.ds(0, 512)], twin_arrived.at[1])
    uf = forward(u_all)
    ur, ui, hr, hi = uf[:, :COLS], uf[:, COLS:], hf[:, :COLS], hf[:, COLS:]
    y = jnp.concatenate([ur * hr - ui * hi, ur * hi + ui * hr], axis=1)
    b = dot3(split(y), (g2[0], g2[1]))
    re, im = b[:, :COLS], b[:, COLS:]
    e = split(jnp.concatenate([re * tw[0] + im * tw[1], im * tw[0] - re * tw[1]], axis=0))
    part_send[...] = dot3((g1[0, HALF:], g1[1, HALF:]), e)
    exchange = pltpu.make_async_remote_copy(
        src_ref=part_send,
        dst_ref=part_all,
        send_sem=part_out,
        recv_sem=part_arrived,
        device_id=(twin, g),
        device_id_type=MESH,
    )
    exchange.start()
    mine = dot3((g1[0, :HALF], g1[1, :HALF]), e)
    exchange.wait()
    mine = mine + part_all[...]
    for bit in range(2):
        for side in range(2):
            y_send[:, 2 * bit + side, :] = mine[128 * bit : 128 * bit + 128, 128 * side : 128 * side + 128]

    spot = chip * GROUPS + g
    channel = g * CHIPS + chip

    pl.semaphore_wait(ready, GROUPS - 1)

    @pl.loop(1, CHIPS * GROUPS, unroll=4)
    def _(d):
        step = jnp.where(d <= 64, 2 * d - 1, 2 * (d - 64))
        to = lax.rem(spot + step, CHIPS * GROUPS)
        pltpu.make_async_remote_copy(
            src_ref=y_send.at[to],
            dst_ref=y_all.at[channel],
            send_sem=y_out,
            recv_sem=y_arrived,
            device_id=(2 * lax.div(to, GROUPS) + core, lax.rem(to, GROUPS)),
            device_id_type=MESH,
        ).start()

    y_own = pltpu.make_async_copy(y_send.at[spot], y_all.at[channel], own_sem.at[1])
    y_own.start()
    wait_bytes(h_send.at[pl.ds(0, 480)], h_out)
    wait_bytes(u_send.at[pl.ds(0, 480)], u_out)
    wait_bytes(h_all.at[pl.ds(0, 512)], twin_out.at[0])
    wait_bytes(u_all.at[pl.ds(0, 512)], twin_out.at[1])
    wait_bytes(q_send.at[pl.ds(0, 112)], q_out)
    wait_bytes(y_send.at[pl.ds(0, CHIPS * GROUPS - 1)], y_out)
    q_own.wait()
    y_own.wait()
    wait_bytes(q_all.at[pl.ds(0, 112)], q_arrived)
    wait_bytes(y_all.at[pl.ds(0, CHIPS * GROUPS - 1)], y_arrived)


def body(query_proj, key_proj, value_proj, filter_taps, skip_bias):
    any_space = pl.BlockSpec(memory_space=pl.ANY)
    dma = pltpu.SemaphoreType.DMA
    consts = [jnp.asarray(t) for t in tables()]
    y, q = pl.pallas_call(
        kernel,
        out_shape=[pltpu.VMEM((128, 4, 128), F32), pltpu.VMEM((128, 512), F32)],
        in_specs=[any_space] * 10,
        out_specs=[any_space] * 2,
        scratch_shapes=[
            pltpu.VMEM((16, 4096), BF16),
            pltpu.VMEM((16, 4096), BF16),
            pltpu.VMEM((16, 4096), BF16),
            pltpu.VMEM((16, 4096), F32),
            pltpu.VMEM((2, ROWS, ROWS), BF16),
            pltpu.VMEM((2, 2 * COLS, 2 * COLS), BF16),
            pltpu.VMEM((2, 2 * COLS, 2 * COLS), BF16),
            pltpu.VMEM((2, ROWS, ROWS), BF16),
            pltpu.VMEM((2, HALF, COLS), F32),
            pltpu.VMEM((512, 128), F32),
            pltpu.VMEM((512, 128), F32),
            pltpu.VMEM((1024, 128), F32),
            pltpu.VMEM((1024, 128), F32),
            pltpu.VMEM((128, 512), F32),
            pltpu.VMEM((128, 4, 128), F32),
            pltpu.VMEM((HALF, COLS), F32),
            pltpu.VMEM((HALF, COLS), F32),
            pltpu.SMEM((CHIPS,), F32),
            dma((10,)),
            dma,
            dma,
            dma((CHIPS,)),
            dma((CHIPS,)),
            dma((2,)),
            dma((2,)),
            dma,
            dma,
            dma,
            dma,
            dma,
            dma,
            pltpu.SemaphoreType.REGULAR,
            dma((2,)),
        ],
        compiler_params=pltpu.CompilerParams(
            collective_id=0, has_side_effects=True, vmem_limit_bytes=107 * 2**19
        ),
        cost_estimate=pl.CostEstimate(flops=2_400_000_000, bytes_accessed=6_000_000, transcendentals=0),
    )(query_proj, key_proj, value_proj, filter_taps, skip_bias, *consts)
    return y.reshape(128, 512) * q


def solution(mesh):
    placed = (P("chan", "seq"), P("chan", "seq"), P("chan", "seq"), P("chan", "seq"), P("chan"))
    return jax.shard_map(
        body, mesh=mesh, in_specs=placed, out_specs=P(None, ("seq", "chan")), check_vma=False
    )
```
